32 devices in a mesh: grp: 2 (over y), exp: 4 (over z), dat: 2 (over x), mdl: 2 (over core).
Axes of the slice: x: 2, y: 2, z: 4, core: 2. Of those that a mesh axis runs over, the one named last changes fastest.
Arguments:
- tokens: bfloat16 [4096, 4096], P(('grp', 'exp', 'dat'), 'mdl'), parts along dimension 0, may hold values from -6 to 6
- cotangent: bfloat16 [4096, 4096], P(('grp', 'exp', 'dat'), 'mdl'), parts along dimension 0, may hold values from -6 to 6
- routes: int32 [4096, 2], P(('grp', 'exp', 'dat')), parts along dimension 0, may hold values from 0 to 3, all different within a row; in each aligned block of 256 rows (0 to 255, 256 to 511, ...) at most 256 rows name the same one
- doc_ids: int32 [16, 256], P(('grp', 'exp', 'dat')), parts along dimension 0, may hold values from 0 to 3, never falling along the last dimension, each value on 1 to 96 neighbouring positions
- gate_weight: bfloat16 [4, 4096, 768], P('exp', 'dat', 'mdl'), may hold values from -0.09375 to 0.09375
- up_weight: bfloat16 [4, 4096, 768], P('exp', 'dat', 'mdl'), may hold values from -0.09375 to 0.09375
- proj_in: bfloat16 [32, 768], P(None, 'mdl'), may hold values from -0.21875 to 0.21875
- proj_out: bfloat16 [32, 4096], P(None, 'mdl'), may hold values from -0.09375 to 0.09375
Outputs:
- grads: float32 [64, 4, 1024], P(('grp', 'exp', 'dat')), parts along dimension 0
The draws below stay inside these ranges and needn't reach their ends.
There are 2 independent parts, one for each index of `grp`. The reference program is written for one: setup_inputs(seed, part) draws one part's arguments, and reference() takes and returns one part's arrays. A program takes and returns all parts, laid end to end along the dimension named above; an argument that names none is the same for every part. Nothing has to cross between parts.
Inputs may be any that keep to these rules, and one draw needn't show every extreme that they name: Each token names 2 different experts; among the tokens of one document shard (aligned blocks of 256 rows) no expert is named by more than 256 routes, and one expert is named by exactly 256. `doc_ids`: each row never falls and holds every document number; a document has at most 96 tokens, and one has exactly that many.
All inputs are finite; a program needn't handle non-finite values.
Results may differ from the reference program's by a relative error of at most 0.0029.
Values may be sent and summed in bfloat16 or wider, within the bound.
No kernel may reach another device: no remote copies, remote signals or barrier semaphores. Data moves between devices by JAX's collectives and lax.ppermute only.
A program may use at most 64 MiB of HBM per device.

```python
import math
import jax
import jax.numpy as jnp
import numpy as np
from jax import lax

D = 4096
FF = 768
RANK = 32
TOPK = 2
DOC_LEN = 64
DOCS_DEV = 4
TOK_DEV = 256
SOURCES = 8
TOKENS = 2048
DOCS = 32
EXPERTS = 4
CAP = 256


def steps_of(rng, shape, pieces, smallest, top_value):
    gain, own = 1.0, jax.random.fold_in(rng, 6)
    for axis_at, shards_of in pieces:
        heights = jnp.exp(jax.random.uniform(jax.random.fold_in(own, axis_at), (shards_of,), jnp.float32, smallest / len(pieces), top_value / len(pieces)))
        gain = gain * jnp.repeat(heights, shape[axis_at] // shards_of).reshape([-1 if axis == axis_at else 1 for axis in range(len(shape))])
    return gain


def length_profile(count, total, reach, lean):
    weights = [(1 << 20) // math.isqrt(rank ** lean) + 1 for rank in range(2, count + 1)]
    surplus, given = total - reach - (count - 1), [1] * (count - 1)
    while surplus > 0:
        movable = [i for i in range(count - 1) if given[i] < reach]
        pool, budget = sum([weights[i] for i in movable]), surplus
        for i in movable:
            addition = min(reach - given[i], max(1, budget * weights[i] // pool), surplus)
            given[i] = given[i] + addition
            surplus = surplus - addition
    return np.array([reach] + given)


def ragged_sizes(key, count, total, bound, slope):
    if count == 2:
        one = jax.random.randint(key, (), max(1, total - bound), min(bound, total - 1) + 1)
        return jnp.stack([one, total - one])
    sizes = jnp.asarray(length_profile(count, total, bound, slope), jnp.int32)
    pairs = (count - 1) // 2
    donor, receiver = sizes[1:1 + 2 * pairs:2], sizes[2:2 + 2 * pairs:2]
    slack = jnp.minimum(donor - 1, bound - receiver)
    shifted = jax.random.randint(jax.random.fold_in(key, 1), (pairs,), 0, 1 << 20) % (slack + 1)
    sizes = sizes.at[1:1 + 2 * pairs:2].set(donor - shifted).at[2:2 + 2 * pairs:2].set(receiver + shifted)
    return sizes[jax.random.permutation(jax.random.fold_in(key, 2), count)]


def routed_block(stream_key, own, number, rows, count, top, limit, skew):
    sequence = jax.random.permutation(stream_key, count)
    packed, usual = shares(count, rows * top, limit, skew, True), shares(count, rows * top, limit, skew, False)
    places = jnp.arange(count)

    def named(tallies, rotation):
        used = int((tallies > 0).sum())
        fixed = max(1, used // 4)
        passed = fixed + (places - fixed + rotation * (used - fixed)) % max(1, count - fixed)
        return jnp.zeros((count,), jnp.int32).at[sequence[jnp.where(places < fixed, places, passed)]].set(jnp.asarray(tallies, jnp.int32))

    tallies = jnp.where(number % 4 == 0, named(packed, number // 4), named(usual, number - number // 4 - 1))
    mixed = jax.random.permutation(jax.random.fold_in(own, 3), count)
    giver, sink = mixed[0:count // 2 * 2:2], mixed[1:count // 2 * 2:2]
    slack = jnp.minimum(tallies[giver] - 1, limit - tallies[sink]) // 2
    slack = jnp.where((giver == sequence[0]) | (sink == sequence[0]) | (tallies[sink] == 0), 0, jnp.maximum(slack, 0))
    passed = jax.random.randint(jax.random.fold_in(own, 4), (count // 2,), 0, 1 << 20) % (slack + 1)
    tallies = tallies.at[giver].add(-passed).at[sink].add(passed)
    items = jnp.searchsorted(jnp.cumsum(tallies), jnp.arange(rows * top), side="right").astype(jnp.int32)
    table = items.reshape(top, rows).T
    table = table[jax.random.permutation(jax.random.fold_in(own, 1), rows)]
    rotation = jax.random.randint(jax.random.fold_in(own, 2), (rows, 1), 0, top)
    return jnp.take_along_axis(table, (jnp.arange(top)[None, :] + rotation) % top, axis=1)


def shares(number_of, total, most, slope, full):
    loads = [(1 << 20) // math.isqrt(grade ** slope) + 1 for grade in range(1, number_of + 1)]
    largest = most if full else min(most, max(-(-total // number_of), total * loads[0] // sum(loads)))
    least = 1 if total - largest >= number_of - 1 else 0
    holding, surplus = [largest] + [least] * (number_of - 1), total - largest - least * (number_of - 1)
    while surplus > 0:
        candidates = [i for i in range(1, number_of) if holding[i] < largest] or [i for i in range(1, number_of) if holding[i] < most]
        mass, left = sum([loads[i] for i in candidates]), surplus
        for i in candidates:
            addition = min(most - holding[i], max(1, left * loads[i] // mass), surplus)
            holding[i] = holding[i] + addition
            surplus = surplus - addition
    return np.array(holding)


def bell_draw(rng, dims, scale, most, pieces=(), kind=jnp.bfloat16):
    drawn = scale * jax.random.normal(rng, dims, jnp.float32)
    if pieces:
        drawn = drawn * steps_of(rng, dims, pieces, -0.22, 0.18)
    return jnp.clip(drawn, -most, most).astype(kind)


def setup_inputs(seed: int = 0, part: int = 0) -> dict:
    key_list = jax.random.split(jax.random.key(seed), 9)
    part_splits = jax.random.split(jax.random.fold_in(key_list[8], part), 9)
    tokens = bell_draw(part_splits[0], (TOKENS, D), 1.0, 6.0, ((0, 8), (1, 2)))
    cotangent = bell_draw(part_splits[1], (TOKENS, D), 1.0, 6.0, ((0, 8), (1, 2)))
    routes_keys = jax.random.split(jax.random.fold_in(part_splits[2], 1), TOKENS // TOK_DEV)
    routes_turns = jax.random.permutation(jax.random.fold_in(part_splits[2], 3), TOKENS // TOK_DEV)
    routes = jax.vmap(lambda own, number: routed_block(jax.random.fold_in(part_splits[2], 2), own, number, TOK_DEV, EXPERTS, TOPK, CAP, 1))(routes_keys, routes_turns).reshape((TOKENS, TOPK))
    doc_ids = jax.vmap(lambda own: jnp.searchsorted(jnp.cumsum(ragged_sizes(own, DOCS_DEV, TOK_DEV, 3 * DOC_LEN // 2, 1)), jnp.arange(TOK_DEV), side="right"))(jax.random.split(part_splits[3], SOURCES)).reshape((SOURCES, TOK_DEV)).astype(jnp.int32)
    gate_weight = bell_draw(key_list[4], (EXPERTS, D, FF), D ** -0.5, 0.09375, ((0, 4), (1, 2), (2, 2)))
    up_weight = bell_draw(key_list[5], (EXPERTS, D, FF), D ** -0.5, 0.09375, ((0, 4), (1, 2), (2, 2)))
    proj_in = bell_draw(key_list[6], (RANK, FF), FF ** -0.5, 0.21875, ((1, 2),))
    proj_out = bell_draw(key_list[7], (RANK, D), D ** -0.5, 0.09375, ((1, 2),))
    return dict(tokens=tokens, cotangent=cotangent, routes=routes, doc_ids=doc_ids, gate_weight=gate_weight, up_weight=up_weight, proj_in=proj_in, proj_out=proj_out)


def expert_codes(row_values, gate_matrix, up_matrix, proj_in):
    gate_pre = jnp.dot(row_values, gate_matrix.astype(jnp.float32), precision=lax.Precision.HIGHEST)
    up_pre = jnp.dot(row_values, up_matrix.astype(jnp.float32), precision=lax.Precision.HIGHEST)
    hidden = (jax.nn.silu(gate_pre) * up_pre).astype(jnp.bfloat16)
    return jnp.dot(hidden.astype(jnp.float32), proj_in.astype(jnp.float32).T, precision=lax.Precision.HIGHEST)


def reference(tokens, cotangent, routes, doc_ids, gate_weight, up_weight, proj_in, proj_out):
    pair_count = TOKENS * TOPK
    most_rows = SOURCES * CAP
    pair_expert = routes.reshape(-1).astype(jnp.int32)
    pair_token = (jnp.arange(pair_count, dtype=jnp.int32) // TOPK).astype(jnp.int32)
    sort_order = jnp.argsort(pair_expert, stable=True).astype(jnp.int32)
    expert_loads = jnp.bincount(pair_expert, length=EXPERTS).astype(jnp.int32)
    starts = (jnp.cumsum(expert_loads) - expert_loads).astype(jnp.int32)
    padded_order = jnp.concatenate([sort_order, jnp.full((most_rows,), pair_count, jnp.int32)])

    def one_expert(expert):
        picked = lax.dynamic_slice_in_dim(padded_order, starts[expert], most_rows).astype(jnp.int32)
        is_valid = jnp.arange(most_rows, dtype=jnp.int32) < expert_loads[expert]
        token_index = pair_token[jnp.minimum(picked, pair_count - 1)]
        row_values = tokens[token_index].astype(jnp.float32)
        code_rows = expert_codes(row_values, gate_weight[expert], up_weight[expert], proj_in)
        targets = jnp.where(is_valid, picked, pair_count).astype(jnp.int32)
        return code_rows, targets

    code_rows, targets = lax.map(one_expert, jnp.arange(EXPERTS, dtype=jnp.int32))
    pair_codes = jnp.zeros((pair_count, RANK), jnp.float32)
    pair_codes = pair_codes.at[targets.reshape(-1)].set(code_rows.reshape(-1, RANK), mode="drop")
    grad_codes = jnp.dot(cotangent, proj_out.T, preferred_element_type=jnp.float32)
    member = (pair_expert[:, None] == jnp.arange(EXPERTS, dtype=jnp.int32)[None, :]).astype(jnp.float32)
    spread = (member[:, :, None] * pair_codes[:, None, :]).reshape(TOKENS, TOPK, EXPERTS * RANK).sum(axis=1)
    spread = spread.reshape(SOURCES, TOK_DEV, EXPERTS * RANK)
    grad_codes = grad_codes.reshape(SOURCES, TOK_DEV, RANK)
    docs_mask = (doc_ids[:, None, :] == jnp.arange(DOCS_DEV, dtype=jnp.int32)[None, :, None]).astype(jnp.float32)
    weighted = docs_mask[:, :, :, None] * grad_codes[:, None, :, :]
    blocks = jnp.einsum("sdti,stf->sdif", weighted, spread, precision=lax.Precision.HIGHEST)
    blocks = blocks.reshape(SOURCES, DOCS_DEV, RANK, EXPERTS, RANK).transpose(0, 1, 3, 2, 4)
    return blocks.reshape(DOCS, EXPERTS, RANK * RANK)
```

```python
import functools

import jax
import jax.numpy as jnp
from jax import lax
from jax.experimental import pallas as pl
from jax.experimental.pallas import tpu as pltpu
from jax.sharding import PartitionSpec as P

DOCS_DEV = 4
CHUNKS = 2
K_BLOCK = 512


def gate_up_kernel(first, last, *refs):
    refs = list(refs)
    mine, other, gate_mine, up_mine, gate_other, up_other = refs[:6]
    refs = refs[6:]
    if not first:
        gate_in, up_in = refs[:2]
        refs = refs[2:]
    if last:
        proj = refs.pop(0)
        out, gate_acc, up_acc = refs
    else:
        gate_acc, up_acc = refs
    step = pl.program_id(0)

    @pl.when(step == 0)
    def _():
        if first:
            gate_acc[...] = jnp.zeros_like(gate_acc)
            up_acc[...] = jnp.zeros_like(up_acc)
        else:
            gate_acc[...] = gate_in[...]
            up_acc[...] = up_in[...]

    x_mine, x_other = mine[...], other[...]
    dot = functools.partial(jnp.dot, preferred_element_type=jnp.float32)
    gate_acc[...] += dot(x_mine, gate_mine[...]) + dot(x_other, gate_other[...])
    up_acc[...] += dot(x_mine, up_mine[...]) + dot(x_other, up_other[...])

    if last:

        @pl.when(step == pl.num_programs(0) - 1)
        def _():
            gate = gate_acc[...]
            hidden = (gate / (1.0 + jnp.exp(-gate)) * up_acc[...]).astype(jnp.bfloat16)
            out[...] = lax.dot_general(
                proj[...], hidden, (((1,), (1,)), ((), ())), preferred_element_type=jnp.float32
            )


def gate_up(mine, other, weights, chunk, sums, proj):
    rows, depth = mine.shape
    cols = weights[0].shape[1]
    first, last = sums is None, proj is not None
    block = min(K_BLOCK, depth)
    steps = depth // block
    base = chunk * steps
    x_spec = pl.BlockSpec((rows, block), lambda i: (0, i))
    w_spec = pl.BlockSpec((block, cols), lambda i: (base + i, 0))
    whole = pl.BlockSpec((rows, cols), lambda i: (0, 0))
    args = [mine, other, *weights]
    in_specs = [x_spec, x_spec] + [w_spec] * 4
    if not first:
        args += list(sums)
        in_specs += [whole, whole]
    acc = jax.ShapeDtypeStruct((rows, cols), jnp.float32)
    if last:
        args.append(proj)
        in_specs.append(pl.BlockSpec(proj.shape, lambda i: (0, 0)))
        out_shape = jax.ShapeDtypeStruct((proj.shape[0], rows), jnp.float32)
        out_specs = pl.BlockSpec(out_shape.shape, lambda i: (0, 0))
        scratch = [pltpu.VMEM((rows, cols), jnp.float32)] * 2
    else:
        out_shape, out_specs, scratch = [acc, acc], [whole, whole], []
    return pl.pallas_call(
        functools.partial(gate_up_kernel, first, last),
        grid=(steps,),
        in_specs=in_specs,
        out_specs=out_specs,
        out_shape=out_shape,
        scratch_shapes=scratch,
        compiler_params=pltpu.CompilerParams(vmem_limit_bytes=24 * 2**20),
        cost_estimate=pl.CostEstimate(
            flops=8 * rows * depth * cols,
            bytes_accessed=4 * rows * depth + 8 * depth * cols,
            transcendentals=rows * cols,
        ),
        name="gate_up",
    )(*args)


def grads_kernel(experts, where, grad_mine, grad_other, docs, routes, *refs):
    same, cross, out = refs[:experts], refs[experts : 2 * experts], refs[2 * experts]
    exact = functools.partial(
        lax.dot_general, precision=lax.Precision.HIGHEST, preferred_element_type=jnp.float32
    )
    rank = grad_mine.shape[0]
    home = where[0]
    grad = grad_mine[...] + grad_other[...]
    left = jnp.concatenate(
        [jnp.where(docs[...] == d, grad, 0.0) for d in range(DOCS_DEV)], axis=0
    )
    row = lax.broadcasted_iota(jnp.int32, (rank, rank * rank), 0)
    lane = lax.broadcasted_iota(jnp.int32, (rank, rank * rank), 1)
    tile = (row == lane % rank).astype(jnp.float32)
    keep = row == lane // rank
    for k in range(experts):
        expert = lax.rem(home + k, experts)
        named = (routes[0:1, :] == expert) | (routes[1:2, :] == expert)
        codes = jnp.where(named, same[k][...] + cross[k][...], 0.0)
        block = exact(left, codes, (((1,), (1,)), ((), ())))
        spread = exact(block, tile, (((1,), (0,)), ((), ())))
        for d in range(DOCS_DEV):
            part = jnp.where(keep, spread[d * rank : (d + 1) * rank], 0.0)
            out[d, pl.ds(expert, 1), :] = jnp.sum(part, axis=0, keepdims=True)


def on_device(tokens, cotangent, routes, doc_ids, gate_weight, up_weight, proj_in, proj_out):
    experts, dats = lax.axis_size("exp"), lax.axis_size("dat")
    home, dat = lax.axis_index("exp"), lax.axis_index("dat")
    core, grp = lax.axis_index("mdl"), lax.axis_index("grp")
    rank = proj_in.shape[0]
    swap = [(0, 1), (1, 0)]
    gate, up = gate_weight[0], up_weight[0]

    width = tokens.shape[1] // CHUNKS
    mine = [[tokens[:, j * width : (j + 1) * width] for j in range(CHUNKS)]]
    ring = [(i, (i + 1) % experts) for i in range(experts)]
    for _ in range(1, experts):
        mine.append([lax.ppermute(x, "exp", ring) for x in mine[-1]])
    other = [[lax.ppermute(x, "mdl", swap) for x in xs] for xs in mine]

    half = jnp.where(grp == 0, gate, up)
    gates, ups = [gate], [up]
    for k in range(1, dats):
        direct = lax.ppermute(half, "dat", [((i + k) % dats, i) for i in range(dats)])
        swapped = lax.ppermute(direct, "grp", swap)
        gates.append(jnp.where(grp == 0, direct, swapped))
        ups.append(jnp.where(grp == 0, swapped, direct))
    per = dats // 2

    def half_of(slots, which):
        blocks = [
            lax.select_n((which * per + i - dat) % dats == 0, slots[1], slots[0])
            if dats == 2
            else lax.select_n((which * per + i - dat) % dats, *slots)
            for i in range(per)
        ]
        return blocks[0] if per == 1 else jnp.concatenate(blocks, axis=0)

    weights = (
        half_of(gates, core),
        half_of(ups, core),
        half_of(gates, 1 - core),
        half_of(ups, 1 - core),
    )

    grad_mine = lax.dot_general(
        proj_out, cotangent, (((1,), (1,)), ((), ())), preferred_element_type=jnp.float32
    )
    grad_other = lax.ppermute(grad_mine, "mdl", swap)

    same, cross = [], []
    for k in range(experts):
        sums = None
        for j in range(CHUNKS):
            last = j == CHUNKS - 1
            sums = gate_up(mine[k][j], other[k][j], weights, j, sums, proj_in if last else None)
        codes = sums
        back = [
            [
                (z * 2 + c, (z - k) % experts * 2 + (c ^ flip))
                for z in range(experts)
                for c in range(2)
            ]
            for flip in range(2)
        ]
        same.append(codes if k == 0 else lax.ppermute(codes, ("exp", "mdl"), back[0]))
        cross.append(lax.ppermute(codes, ("exp", "mdl"), back[1]))

    tok_count = tokens.shape[0]
    vmem = pl.BlockSpec(memory_space=pltpu.VMEM)
    return pl.pallas_call(
        functools.partial(grads_kernel, experts),
        in_specs=[pl.BlockSpec(memory_space=pltpu.SMEM)] + [vmem] * (4 + 2 * experts),
        out_specs=vmem,
        out_shape=jax.ShapeDtypeStruct((DOCS_DEV, experts, rank * rank), jnp.float32),
        compiler_params=pltpu.CompilerParams(vmem_limit_bytes=24 * 2**20),
        cost_estimate=pl.CostEstimate(
            flops=2 * experts * DOCS_DEV * rank * rank * tok_count,
            bytes_accessed=2**20,
            transcendentals=0,
        ),
        name="doc_grads",
    )(home.reshape(1), grad_mine, grad_other, doc_ids, routes.T, *same, *cross)


def solution(mesh):
    placed = (
        P(("grp", "exp", "dat"), "mdl"),
        P(("grp", "exp", "dat"), "mdl"),
        P(("grp", "exp", "dat"), None),
        P(("grp", "exp", "dat"), None),
        P("exp", "dat", "mdl"),
        P("exp", "dat", "mdl"),
        P(None, "mdl"),
        P(None, "mdl"),
    )
    return jax.shard_map(
        on_device,
        mesh=mesh,
        in_specs=placed,
        out_specs=P(("grp", "exp", "dat"), None, None),
        check_vma=False,
    )
```

```python
import functools

import jax
import jax.numpy as jnp
from jax import lax
from jax.experimental import pallas as pl
from jax.experimental.pallas import tpu as pltpu
from jax.sharding import PartitionSpec as P

DOCS_DEV = 4
CHUNKS = 2
LANES = 128


def after(x, *others):
    place = pl.BlockSpec(memory_space=pl.ANY)
    return pl.pallas_call(
        lambda *refs: None,
        in_specs=[place] * (1 + len(others)),
        out_specs=place,
        out_shape=jax.ShapeDtypeStruct(x.shape, x.dtype),
        input_output_aliases={0: 0},
        name="after",
    )(x, *others)


def gate_up_kernel(first, last, mine, other, mine_weights, other_weights, *refs):
    dot = functools.partial(jnp.dot, preferred_element_type=jnp.float32)
    total = dot(mine[...], mine_weights[...]) + dot(other[...], other_weights[...])
    if not first:
        total = total + refs[0][...]
    out = refs[-1]
    if not last:
        out[...] = total
        return
    cols = total.shape[1] // 2
    gate, up = total[:, :cols], total[:, cols:]
    hidden = (gate / (1.0 + jnp.exp(-gate)) * up).astype(jnp.bfloat16)
    proj = refs[-2]
    out[...] = lax.dot_general(
        proj[...], hidden, (((1,), (1,)), ((), ())), preferred_element_type=jnp.float32
    )


def gate_up(mine, other, weights, total, proj):
    rows, depth = mine.shape
    cols = weights[0].shape[1]
    first, last = total is None, proj is not None
    args = [mine, other, *weights]
    args += [] if first else [total]
    args += [proj] if last else []
    vmem = pl.BlockSpec(memory_space=pltpu.VMEM)
    shape = (proj.shape[0], rows) if last else (rows, cols)
    return pl.pallas_call(
        functools.partial(gate_up_kernel, first, last),
        in_specs=[vmem] * len(args),
        out_specs=vmem,
        out_shape=jax.ShapeDtypeStruct(shape, jnp.float32),
        compiler_params=pltpu.CompilerParams(vmem_limit_bytes=24 * 2**20),
        cost_estimate=pl.CostEstimate(
            flops=4 * rows * depth * cols,
            bytes_accessed=4 * rows * depth + 4 * depth * cols,
            transcendentals=rows * cols // 2 if last else 0,
        ),
        name="gate_up",
    )(*args)


def grads_kernel(experts, where, grad_mine, grad_other, docs, routes, *refs):
    same, cross = refs[:experts], refs[experts : 2 * experts]
    out, by_expert = refs[2 * experts :]
    rank = grad_mine.shape[0]
    group = LANES // rank
    long = rank // group
    home = where[0]
    grad = grad_mine[...] + grad_other[...]
    masks = [docs[...] == d for d in range(DOCS_DEV)]
    left = jnp.concatenate(
        [
            jnp.where(mask, grad[q * long : (q + 1) * long], 0.0)
            for q in range(group)
            for mask in masks
        ],
        axis=0,
    )
    for k in range(experts):
        by_expert[lax.rem(home + k, experts)] = same[k][...] + cross[k][...]
    for expert in range(experts):
        named = (routes[0:1, :] == expert) | (routes[1:2, :] == expert)
        codes = jnp.where(named, by_expert[expert], 0.0)
        block = lax.dot_general(
            left,
            codes,
            (((1,), (1,)), ((), ())),
            precision=lax.Precision.HIGHEST,
            preferred_element_type=jnp.float32,
        )
        rows = DOCS_DEV * long
        wide = jnp.concatenate(
            [block[q * rows : (q + 1) * rows] for q in range(group)], axis=1
        )
        for d in range(DOCS_DEV):
            for i in range(long):
                at = d * long + i
                out[d, expert : expert + 1, i * LANES : (i + 1) * LANES] = wide[at : at + 1]


def on_device(tokens, cotangent, routes, doc_ids, gate_weight, up_weight, proj_in, proj_out):
    experts, dats = lax.axis_size("exp"), lax.axis_size("dat")
    home, dat = lax.axis_index("exp"), lax.axis_index("dat")
    core, grp = lax.axis_index("mdl"), lax.axis_index("grp")
    rank, half = proj_in.shape[0], tokens.shape[1]
    swap = [(0, 1), (1, 0)]
    gate, up = gate_weight[0], up_weight[0]

    width = half // CHUNKS
    mine = [[tokens[:, j * width : (j + 1) * width] for j in range(CHUNKS)]]
    ring = [(i, (i + 1) % experts) for i in range(experts)]
    for _ in range(1, experts):
        mine.append([lax.ppermute(x, "exp", ring) for x in mine[-1]])
    other = [[lax.ppermute(x, "mdl", swap) for x in xs] for xs in mine]

    block = gate.shape[0]
    piece = min(block, width)
    held = [[] for _ in range(block // piece)]
    for i, slots in enumerate(held):
        rows = slice(i * piece, (i + 1) * piece)
        gate_own, up_own = gate[rows], up[rows]
        slots.append(jnp.concatenate([gate_own, up_own], axis=1))
        sent = jnp.where(grp == 0, gate_own, up_own)
        for k in range(1, dats):
            direct = lax.ppermute(sent, "dat", [((z + k) % dats, z) for z in range(dats)])
            if dats == 2 and experts > 2 and i < 2:
                direct = after(direct, mine[1][1] if i == 0 else mine[2][0])
            swapped = lax.ppermute(direct, "grp", swap)
            slots.append(
                jnp.concatenate(
                    [
                        jnp.where(grp == 0, direct, swapped),
                        jnp.where(grp == 0, swapped, direct),
                    ],
                    axis=1,
                )
            )

    def rows_of(which, chunk):
        found = []
        for at in range(chunk * width, (chunk + 1) * width, piece):
            slot = (which * (half // block) + at // block - dat) % dats
            slots = held[at % block // piece]
            found.append(lax.select_n(slot == 1 if dats == 2 else slot, *slots))
        return found[0] if len(found) == 1 else jnp.concatenate(found, axis=0)

    weights = [(rows_of(core, j), rows_of(1 - core, j)) for j in range(CHUNKS)]

    group = LANES // rank
    ordered = proj_out.reshape(rank // group, group, half).transpose(1, 0, 2).reshape(rank, half)
    grad_mine = lax.dot_general(
        ordered, cotangent, (((1,), (1,)), ((), ())), preferred_element_type=jnp.float32
    )
    grad_other = lax.ppermute(grad_mine, "mdl", swap)

    same, cross = [], []
    for k in range(experts):
        total = None
        for j in range(CHUNKS):
            last = j == CHUNKS - 1
            total = gate_up(mine[k][j], other[k][j], weights[j], total, proj_in if last else None)
        back = [
            [
                (z * 2 + c, (z - k) % experts * 2 + (c ^ flip))
                for z in range(experts)
                for c in range(2)
            ]
            for flip in range(2)
        ]
        same.append(total if k == 0 else lax.ppermute(total, ("exp", "mdl"), back[0]))
        cross.append(lax.ppermute(total, ("exp", "mdl"), back[1]))

    tok_count = tokens.shape[0]
    vmem = pl.BlockSpec(memory_space=pltpu.VMEM)
    return pl.pallas_call(
        functools.partial(grads_kernel, experts),
        in_specs=[pl.BlockSpec(memory_space=pltpu.SMEM)] + [vmem] * (4 + 2 * experts),
        out_specs=vmem,
        out_shape=jax.ShapeDtypeStruct((DOCS_DEV, experts, rank * rank), jnp.float32),
        scratch_shapes=[pltpu.VMEM((experts, rank, tok_count), jnp.float32)],
        compiler_params=pltpu.CompilerParams(vmem_limit_bytes=24 * 2**20),
        cost_estimate=pl.CostEstimate(
            flops=2 * experts * DOCS_DEV * rank * rank * tok_count,
            bytes_accessed=2**20,
            transcendentals=0,
        ),
        name="doc_grads",
    )(home.reshape(1), grad_mine, grad_other, doc_ids, routes.T, *same, *cross)


def solution(mesh):
    placed = (
        P(("grp", "exp", "dat"), "mdl"),
        P(("grp", "exp", "dat"), "mdl"),
        P(("grp", "exp", "dat"), None),
        P(("grp", "exp", "dat"), None),
        P("exp", "dat", "mdl"),
        P("exp", "dat", "mdl"),
        P(None, "mdl"),
        P(None, "mdl"),
    )
    return jax.shard_map(
        on_device,
        mesh=mesh,
        in_specs=placed,
        out_specs=P(("grp", "exp", "dat"), None, None),
        check_vma=False,
    )
```

```python
import functools

import jax
import jax.numpy as jnp
from jax import lax
from jax.experimental import pallas as pl
from jax.experimental.pallas import tpu as pltpu
from jax.sharding import PartitionSpec as P

DOCS_DEV = 4
SPLIT = (7, 9)
LANES = 128
GROUP = 3
WAVES = (9, 9, 8, 6)
PIN_BYTES = 24 * 2**20
FREE = pl.CostEstimate(flops=1, bytes_accessed=1, transcendentals=0)


def in_hbm(xs):
    pinned = lax.axis_size("exp") * 2**21 <= PIN_BYTES
    return [pltpu.with_memory_space_constraint(x, pltpu.HBM) if pinned else x for x in xs]


def ordered(turn, arrays, others=(), pin=True):
    hbm = pl.BlockSpec(memory_space=pltpu.HBM)
    kept = [turn, *arrays]
    pin = pin and lax.axis_size("exp") * 2**21 <= PIN_BYTES
    make = pltpu.HBM if pin else jax.ShapeDtypeStruct
    out = pl.pallas_call(
        lambda *refs: None,
        in_specs=[hbm] * len(kept) + [pl.BlockSpec(memory_space=pltpu.VMEM)] * len(others),
        out_specs=[hbm] * len(kept),
        out_shape=[make(x.shape, x.dtype) for x in kept],
        input_output_aliases={i: i for i in range(len(kept))},
        compiler_params=pltpu.CompilerParams(vmem_limit_bytes=2**20),
        name="ordered",
    )(*(in_hbm(kept) if pin else kept), *others)
    return out[0], list(out[1:])


def join_kernel(dats, edges, where, gate, up, *refs):
    pieces = len(edges) - 1
    count = (dats - 1) * pieces
    direct, swapped = refs[:count], refs[count : 2 * count]
    out, sem = refs[2 * count :]
    core, dat, grp = where[0], where[1], where[2]
    cols = gate.shape[1]
    per = dats // 2

    def at(k, i, upper):
        block = lax.rem(dat + k, dats)
        side = jnp.where(lax.div(block, per) == core, 0, 1)
        lanes = pl.ds(pl.multiple_of(upper * cols, LANES), cols)
        rows = pl.ds(edges[i] - edges[0], edges[i + 1] - edges[i])
        return out.at[side * per + lax.rem(block, per), rows, lanes]

    moves = []
    for i in range(pieces):
        rows = pl.ds(edges[i], edges[i + 1] - edges[i])
        moves += [(gate.at[rows], at(0, i, 0)), (up.at[rows], at(0, i, 1))]
        for k in range(1, dats):
            index = i * (dats - 1) + k - 1
            moves += [(direct[index], at(k, i, grp)), (swapped[index], at(k, i, 1 - grp))]
    copies = [pltpu.make_async_copy(a, b, sem.at[i]) for i, (a, b) in enumerate(moves)]
    for copy in copies:
        copy.start()
    for copy in copies:
        copy.wait()


def join(where, gate, up, direct, swapped, dats, edges):
    hbm, vmem = pl.BlockSpec(memory_space=pltpu.HBM), pl.BlockSpec(memory_space=pltpu.VMEM)
    return pl.pallas_call(
        functools.partial(join_kernel, dats, edges),
        in_specs=[pl.BlockSpec(memory_space=pltpu.SMEM)] + [hbm] * (2 + 2 * len(direct)),
        out_specs=vmem,
        out_shape=jax.ShapeDtypeStruct((dats, edges[-1] - edges[0], 2 * gate.shape[1]), gate.dtype),
        scratch_shapes=[pltpu.SemaphoreType.DMA((2 * (len(edges) - 1) * dats,))],
        compiler_params=pltpu.CompilerParams(vmem_limit_bytes=8 * 2**20),
        cost_estimate=FREE,
        name="join",
    )(where, *in_hbm([gate, up, *direct, *swapped]))


def gated(total):
    cols = total.shape[1] // 2
    gate, up = total[:, :cols], total[:, cols:]
    return (gate / (1.0 + jnp.exp(-gate)) * up).astype(jnp.bfloat16)


def segments(low, high, block, cut):
    found, at = [], low
    while at < high:
        start, off = at // block * block, at % block
        part = int(off >= cut)
        end = min(high, start + (block if part else cut))
        found.append((at, end, part, at // block, off - part * cut))
        at = end
    return found


def gate_up_dot(x_of, low, high, size, weights, total=None, parts=(0, 1)):
    per = weights[0].shape[0] // 2
    for start, end, part, block, row in segments(low, high, size, weights[0].shape[1]):
        if part in parts:
            for side in range(2):
                rows = weights[part][side * per + block, row : row + end - start]
                piece = jnp.dot(x_of(side, start, end), rows, preferred_element_type=jnp.float32)
                total = piece if total is None else total + piece
    return total


def codes_of(hidden, proj):
    return lax.dot_general(
        proj[...], hidden, (((1,), (1,)), ((), ())), preferred_element_type=jnp.float32
    )


def shards_kernel(spans, size, first, opened, shards, *refs):
    count = len(spans)
    refs = list(refs)
    sources = [refs.pop(0) for _ in range(2 * count * shards)]
    weights = [refs.pop(0) for _ in range(1 if first else 2)]
    sums = None if first or not opened else refs.pop(0)
    proj = None if first else refs.pop(0)
    out, held_early, held_late, sem = refs
    cut, per = weights[0].shape[1], weights[0].shape[0] // 2

    def copies(n):
        slot, at = n % 2, 0
        taken = (0,) if first else (1,) if n < opened else (0, 1)
        for i, (low, high) in enumerate(spans):
            for start, end, part, block, row in segments(low, high, size, cut):
                for side in range(2) if part in taken else ():
                    place = (side * per + block) * (size - cut if part else cut) + row
                    yield pltpu.make_async_copy(
                        sources[(2 * n + side) * count + i].at[:, pl.ds(start - low, end - start)],
                        (held_early, held_late)[part].at[slot, :, pl.ds(place, end - start)],
                        sem.at[slot, at],
                    )
                    at += 1

    def times(x, part):
        rows = weights[part][...]
        rows = rows.reshape(rows.shape[0] * rows.shape[1], rows.shape[2])
        return jnp.dot(x[...], rows, preferred_element_type=jnp.float32)

    for copy in copies(0):
        copy.start()
    for n in range(shards):
        for copy in copies(n):
            copy.wait()
        if n + 1 < shards:
            for copy in copies(n + 1):
                copy.start()
        if first:
            out[n] = times(held_early.at[n % 2], 0)
        else:
            total = sums[n] if n < opened else times(held_early.at[n % 2], 0)
            out[n] = codes_of(gated(total + times(held_late.at[n % 2], 1)), proj)


def part_kernel(span, size, first, last, mine, other, early, late, *refs):
    x_of = lambda side, start, end: (mine, other)[side][:, start - span[0] : end - span[0]]
    total = gate_up_dot(x_of, *span, size, (early, late), None if first else refs[0][...])
    refs[-1][...] = codes_of(gated(total), refs[-2]) if last else total


def vmem_call(kernel, args, shape, name, far=0, scratch=()):
    vmem, hbm = pl.BlockSpec(memory_space=pltpu.VMEM), pl.BlockSpec(memory_space=pltpu.HBM)
    return pl.pallas_call(
        kernel,
        in_specs=[hbm] * far + [vmem] * (len(args) - far),
        out_specs=vmem,
        out_shape=jax.ShapeDtypeStruct(shape, jnp.float32),
        scratch_shapes=scratch,
        compiler_params=pltpu.CompilerParams(vmem_limit_bytes=20 * 2**20),
        cost_estimate=FREE,
        name=name,
    )(*in_hbm(args[:far]), *args[far:])


def grads_kernel(experts, where, grad_mine, grad_other, docs, routes, *refs):
    codes_of_step, (cross, out, by_expert) = refs[:experts], refs[experts:]
    rank = grad_mine.shape[0]
    group = LANES // rank
    long = rank // group
    home = where[0]
    grad = grad_mine[...] + grad_other[...]
    masks = [docs[...] == d for d in range(DOCS_DEV)]
    left = jnp.concatenate(
        [
            jnp.where(mask, grad[q * long : (q + 1) * long], 0.0)
            for q in range(group)
            for mask in masks
        ],
        axis=0,
    )
    for k in range(experts):
        codes = codes_of_step[k][...]
        by_expert[lax.rem(home + k, experts)] = codes if k < experts - 1 else codes + cross[...]
    for expert in range(experts):
        named = (routes[0:1, :] == expert) | (routes[1:2, :] == expert)
        codes = jnp.where(named, by_expert[expert], 0.0)
        block = lax.dot_general(
            left,
            codes,
            (((1,), (1,)), ((), ())),
            precision=lax.Precision.HIGHEST,
            preferred_element_type=jnp.float32,
        )
        rows = DOCS_DEV * long
        wide = jnp.concatenate(
            [block[q * rows : (q + 1) * rows] for q in range(group)], axis=1
        )
        for d in range(DOCS_DEV):
            for i in range(long):
                at = d * long + i
                out[d, expert : expert + 1, i * LANES : (i + 1) * LANES] = wide[at : at + 1]


def on_device(tokens, cotangent, routes, doc_ids, gate_weight, up_weight, proj_in, proj_out):
    experts, dats = lax.axis_size("exp"), lax.axis_size("dat")
    home, dat = lax.axis_index("exp"), lax.axis_index("dat")
    core, grp = lax.axis_index("mdl"), lax.axis_index("grp")
    rank, half = proj_in.shape[0], tokens.shape[1]
    swap = [(0, 1), (1, 0)]
    gate, up = gate_weight[0], up_weight[0]

    group = LANES // rank
    reordered = proj_out.reshape(rank // group, group, half).transpose(1, 0, 2)
    grad_mine = lax.dot_general(
        reordered.reshape(rank, half),
        cotangent,
        (((1,), (1,)), ((), ())),
        preferred_element_type=jnp.float32,
    )
    grad_other = lax.ppermute(grad_mine, "mdl", swap)

    unit = half // sum(SPLIT)
    edges = [unit * sum(SPLIT[:j]) for j in range(len(SPLIT) + 1)]
    chunks = list(zip(edges, edges[1:]))
    count = len(chunks)
    ring = [(i, (i + 1) % experts) for i in range(experts)]
    held = [tokens[:, low:high] for low, high in chunks]
    mine, other = [held], [[lax.ppermute(x, "mdl", swap) for x in held]]

    block = gate.shape[0]
    row_edges = [0]
    for share in WAVES:
        row_edges.append(row_edges[-1] + block * share // sum(WAVES) // 16 * 16)
    row_edges[-2:] = [row_edges[-2] // LANES * LANES, block]
    sent = [
        jnp.where(grp == 0, gate[low:high], up[low:high])
        for low, high in zip(row_edges, row_edges[1:])
    ]
    waves = [[x] for x in sent]

    def along_dat(xs):
        return [
            lax.ppermute(x, "dat", [((z + k) % dats, z) for z in range(dats)])
            for x in xs
            for k in range(1, dats)
        ]

    def over_grp(xs):
        return [lax.ppermute(x, "grp", swap) for x in xs]

    arriving, swapping = along_dat(waves[0]), []
    direct, swapped = [], []

    turn = jnp.zeros((8, LANES), jnp.float32)
    exchanged, flat, wave = [[], other[0]], [], 0
    for step in range(1, experts):
        moved = [lax.ppermute(x, "exp", ring) for x in mine[-1]]
        mine.append(moved)
        if step == experts - 1:
            break
        for j in range(count):
            wave += 1
            late = waves[wave] if wave < len(waves) else []
            ready = exchanged.pop(0)
            sizes = [1, len(ready), len(arriving), len(swapping), len(late)]
            turn, got = ordered(turn, [moved[j], *ready, *arriving, *swapping, *late])
            got = [got[sum(sizes[:n]) : sum(sizes[: n + 1])] for n in range(len(sizes))]
            moved[j] = got[0][0]
            flat += got[1]
            direct += got[2]
            swapped += got[3]
            swapping, arriving = over_grp(got[2]), along_dat(got[4])
            exchanged.append([lax.ppermute(moved[j], "mdl", swap)])
    where = jnp.stack([core, dat, grp]).astype(jnp.int32)
    some = (len(waves) - 1) * (dats - 1)
    early = join(where, gate, up, direct[:some], swapped[:some], dats, row_edges[:-1])

    def shards_call(low, high, opened, weights, more, shape):
        first = len(weights) == 1
        args = [x for k in range(low, high) for x in (*mine[k], *other[k])]
        cut = row_edges[-2]
        pieces = sum(len(segments(*span, block, cut)) for span in chunks)
        return vmem_call(
            functools.partial(shards_kernel, chunks, block, first, opened, high - low),
            [*args, *weights, *more],
            (high - low, *shape),
            "shards",
            len(args),
            [
                pltpu.VMEM((2, tokens.shape[0], dats * cut), tokens.dtype),
                pltpu.VMEM((2, tokens.shape[0], dats * (block - cut)), tokens.dtype),
                pltpu.SemaphoreType.DMA((2, 2 * pieces)),
            ],
        )

    other = [flat[n : n + count] for n in range(0, len(flat), count)]
    begun = []
    for low in range(0, experts - 2, GROUP):
        high = min(low + GROUP, experts - 2)
        begun.append(
            shards_call(
                low, high, 0, (early,), (), (tokens.shape[0], early.shape[2])
            )
        )

    ready = exchanged.pop(0)
    turn, got = ordered(
        turn, [mine[-1][0], *ready, *swapping], [x[0, :8, :LANES] for x in begun]
    )
    mine[-1][0] = got[0]
    flat += got[1 : 1 + len(ready)] + exchanged.pop(0)
    swapped += got[1 + len(ready) :]
    other = [flat[n : n + count] for n in range(0, len(flat), count)]
    late = join(where, gate, up, direct[some:], swapped[some:], dats, row_edges[-2:])
    weights = (early, late)

    codes = []
    groups = [(n, min(n + GROUP, experts - 2)) for n in range(0, experts - 2, GROUP)]
    for low, high in [*groups, (experts - 2, experts - 1)]:
        opened = min(high, experts - 2) - low
        found = shards_call(
            low,
            high,
            opened,
            weights,
            (*begun[low // GROUP :][: int(opened > 0)], proj_in),
            (rank, tokens.shape[0]),
        )
        found = found + lax.ppermute(found, "mdl", swap)
        for k in range(low, high):
            back = [(z, (z - k) % experts) for z in range(experts)]
            codes.append(found[0] if k == 0 else lax.ppermute(found[k - low], "exp", back))

    made, total = [grad_other, codes[0], found[0]], None
    for j in range(count):
        last = j == count - 1
        turn, (x,) = ordered(turn, [mine[-1][j]], made, False) if j else (turn, [mine[-1][j]])
        args = [x, lax.ppermute(x, "mdl", swap), *weights]
        args += [] if total is None else [total]
        args += [proj_in] if last else []
        total = vmem_call(
            functools.partial(part_kernel, chunks[j], block, total is None, last),
            args,
            (rank, tokens.shape[0]) if last else (tokens.shape[0], early.shape[2]),
            "part",
        )
        made += [total[:8, :LANES]]
    home_pairs = [
        [
            (z * 2 + c, (z + 1) % experts * 2 + (c ^ flip))
            for z in range(experts)
            for c in range(2)
        ]
        for flip in range(2)
    ]
    codes.append(lax.ppermute(total, ("exp", "mdl"), home_pairs[0]))
    cross = lax.ppermute(total, ("exp", "mdl"), home_pairs[1])

    tok_count = tokens.shape[0]
    vmem = pl.BlockSpec(memory_space=pltpu.VMEM)
    return pl.pallas_call(
        functools.partial(grads_kernel, experts),
        in_specs=[pl.BlockSpec(memory_space=pltpu.SMEM)] + [vmem] * (5 + experts),
        out_specs=vmem,
        out_shape=jax.ShapeDtypeStruct((DOCS_DEV, experts, rank * rank), jnp.float32),
        scratch_shapes=[pltpu.VMEM((experts, rank, tok_count), jnp.float32)],
        compiler_params=pltpu.CompilerParams(vmem_limit_bytes=4 * 2**20),
        cost_estimate=pl.CostEstimate(
            flops=2 * experts * DOCS_DEV * rank * rank * tok_count,
            bytes_accessed=2**20,
            transcendentals=0,
        ),
        name="doc_grads",
    )(home.reshape(1), grad_mine, grad_other, doc_ids, routes.T, *codes, cross)


def solution(mesh):
    placed = (
        P(("grp", "exp", "dat"), "mdl"),
        P(("grp", "exp", "dat"), "mdl"),
        P(("grp", "exp", "dat"), None),
        P(("grp", "exp", "dat"), None),
        P("exp", "dat", "mdl"),
        P("exp", "dat", "mdl"),
        P(None, "mdl"),
        P(None, "mdl"),
    )
    return jax.shard_map(
        on_device,
        mesh=mesh,
        in_specs=placed,
        out_specs=P(("grp", "exp", "dat"), None, None),
        check_vma=False,
    )
```

```python
import functools

import jax
import jax.numpy as jnp
from jax import lax
from jax.experimental import pallas as pl
from jax.experimental.pallas import tpu as pltpu
from jax.sharding import PartitionSpec as P

DOCS_DEV = 4
SPLIT = (7, 9)
LANES = 128
GROUP = 3
WAVES = (9, 9, 8, 6)
CUTS = (3, 4)
PIN_BYTES = 24 * 2**20
FREE = pl.CostEstimate(flops=1, bytes_accessed=1, transcendentals=0)


def in_hbm(xs):
    pinned = lax.axis_size("exp") * 2**21 <= PIN_BYTES
    return [pltpu.with_memory_space_constraint(x, pltpu.HBM) if pinned else x for x in xs]


def ordered(turn, arrays, others=(), pin=True):
    hbm = pl.BlockSpec(memory_space=pltpu.HBM)
    kept = [turn, *arrays]
    pin = pin and lax.axis_size("exp") * 2**21 <= PIN_BYTES
    make = pltpu.HBM if pin else jax.ShapeDtypeStruct
    out = pl.pallas_call(
        lambda *refs: None,
        in_specs=[hbm] * len(kept) + [pl.BlockSpec(memory_space=pltpu.VMEM)] * len(others),
        out_specs=[hbm] * len(kept),
        out_shape=[make(x.shape, x.dtype) for x in kept],
        input_output_aliases={i: i for i in range(len(kept))},
        compiler_params=pltpu.CompilerParams(vmem_limit_bytes=2**20),
        name="ordered",
    )(*(in_hbm(kept) if pin else kept), *others)
    return out[0], list(out[1:])


def join_kernel(dats, edges, where, gate, up, *refs):
    pieces = len(edges) - 1
    count = (dats - 1) * pieces
    direct, swapped = refs[:count], refs[count : 2 * count]
    out, sem = refs[2 * count :]
    core, dat, grp = where[0], where[1], where[2]
    cols = gate.shape[1]
    per = dats // 2

    def at(k, i, upper):
        block = lax.rem(dat + k, dats)
        side = jnp.where(lax.div(block, per) == core, 0, 1)
        lanes = pl.ds(pl.multiple_of(upper * cols, LANES), cols)
        rows = pl.ds(edges[i] - edges[0], edges[i + 1] - edges[i])
        return out.at[side * per + lax.rem(block, per), rows, lanes]

    moves = []
    for i in range(pieces):
        rows = pl.ds(edges[i], edges[i + 1] - edges[i])
        moves += [(gate.at[rows], at(0, i, 0)), (up.at[rows], at(0, i, 1))]
        for k in range(1, dats):
            index = i * (dats - 1) + k - 1
            moves += [(direct[index], at(k, i, grp)), (swapped[index], at(k, i, 1 - grp))]
    copies = [pltpu.make_async_copy(a, b, sem.at[i]) for i, (a, b) in enumerate(moves)]
    for copy in copies:
        copy.start()
    for copy in copies:
        copy.wait()


def join(where, gate, up, direct, swapped, dats, edges):
    hbm, vmem = pl.BlockSpec(memory_space=pltpu.HBM), pl.BlockSpec(memory_space=pltpu.VMEM)
    return pl.pallas_call(
        functools.partial(join_kernel, dats, edges),
        in_specs=[pl.BlockSpec(memory_space=pltpu.SMEM)] + [hbm] * (2 + 2 * len(direct)),
        out_specs=vmem,
        out_shape=jax.ShapeDtypeStruct((dats, edges[-1] - edges[0], 2 * gate.shape[1]), gate.dtype),
        scratch_shapes=[pltpu.SemaphoreType.DMA((2 * (len(edges) - 1) * dats,))],
        compiler_params=pltpu.CompilerParams(vmem_limit_bytes=8 * 2**20),
        cost_estimate=FREE,
        name="join",
    )(where, *in_hbm([gate, up, *direct, *swapped]))


def gated(total):
    cols = total.shape[1] // 2
    gate, up = total[:, :cols], total[:, cols:]
    return (gate / (1.0 + jnp.exp(-gate)) * up).astype(jnp.bfloat16)


def segments(low, high, cuts):
    found, at, size = [], low, cuts[-1]
    while at < high:
        start, off = at // size * size, at % size
        part = sum(off >= cut for cut in cuts)
        end = min(high, start + cuts[part])
        found.append((at, end, part, at // size, off - (cuts[part - 1] if part else 0)))
        at = end
    return found


def codes_of(hidden, proj):
    return lax.dot_general(
        proj[...], hidden, (((1,), (1,)), ((), ())), preferred_element_type=jnp.float32
    )


def shards_kernel(spans, cuts, plan, opened, last, *refs):
    count, refs = len(spans), list(refs)
    used = sorted({part for taken in plan for part in taken})
    sources = [refs.pop(0) for _ in range(2 * count * len(plan))]
    weights = {part: refs.pop(0) for part in used}
    sums = refs.pop(0) if opened else None
    proj = refs.pop(0) if last else None
    out, sem = refs.pop(0), refs.pop(-1)
    held = dict(zip(used, refs))
    rows, per = sources[0].shape[0], weights[used[0]].shape[0] // 2

    copies, at = {part: [] for part in used}, 0
    for n, taken in enumerate(plan):
        for i, (low, high) in enumerate(spans):
            for start, end, part, block, row in segments(low, high, cuts):
                for side in range(2) if part in taken else ():
                    place = (side * per + block) * weights[part].shape[1] + row
                    copies[part].append(
                        pltpu.make_async_copy(
                            sources[(2 * n + side) * count + i].at[
                                :, pl.ds(start - low, end - start)
                            ],
                            held[part].at[pl.ds(n * rows, rows), pl.ds(place, end - start)],
                            sem.at[at],
                        )
                    )
                    at += 1
    for part in used:
        for copy in copies[part]:
            copy.start()
    totals = [sums[n] if n < opened else None for n in range(len(plan))]
    for part in used:
        for copy in copies[part]:
            copy.wait()
        takers = [n for n, taken in enumerate(plan) if part in taken]
        mat = weights[part][...]
        mat = mat.reshape(mat.shape[0] * mat.shape[1], mat.shape[2])
        x = held[part][takers[0] * rows : (takers[-1] + 1) * rows]
        found = jnp.dot(x, mat, preferred_element_type=jnp.float32)
        for n in takers:
            own = found[(n - takers[0]) * rows : (n - takers[0] + 1) * rows]
            totals[n] = own if totals[n] is None else totals[n] + own
    for n, total in enumerate(totals):
        out[n] = codes_of(gated(total), proj) if last else total


def part_kernel(span, cuts, first, last, mine, other, *refs):
    weights, refs = refs[: len(cuts)], refs[len(cuts) :]
    per, total = weights[0].shape[0] // 2, None if first else refs[0][...]
    for start, end, part, block, row in segments(*span, cuts):
        for side, x in enumerate((mine, other)):
            piece = jnp.dot(
                x[:, start - span[0] : end - span[0]],
                weights[part][side * per + block, row : row + end - start],
                preferred_element_type=jnp.float32,
            )
            total = piece if total is None else total + piece
    refs[-1][...] = codes_of(gated(total), refs[-2]) if last else total


def vmem_call(kernel, args, shape, name, far=0, scratch=()):
    vmem, hbm = pl.BlockSpec(memory_space=pltpu.VMEM), pl.BlockSpec(memory_space=pltpu.HBM)
    return pl.pallas_call(
        kernel,
        in_specs=[hbm] * far + [vmem] * (len(args) - far),
        out_specs=vmem,
        out_shape=jax.ShapeDtypeStruct(shape, jnp.float32),
        scratch_shapes=scratch,
        compiler_params=pltpu.CompilerParams(vmem_limit_bytes=20 * 2**20),
        cost_estimate=FREE,
        name=name,
    )(*args)


def grads_kernel(experts, where, grad_mine, grad_other, docs, routes, *refs):
    codes_of_step, (cross, out, by_expert) = refs[:experts], refs[experts:]
    rank = grad_mine.shape[0]
    group = LANES // rank
    long = rank // group
    home = where[0]
    grad = grad_mine[...] + grad_other[...]
    masks = [docs[...] == d for d in range(DOCS_DEV)]
    left = jnp.concatenate(
        [
            jnp.where(mask, grad[q * long : (q + 1) * long], 0.0)
            for q in range(group)
            for mask in masks
        ],
        axis=0,
    )
    for k in range(experts):
        codes = codes_of_step[k][...]
        by_expert[lax.rem(home + k, experts)] = codes if k < experts - 1 else codes + cross[...]
    for expert in range(experts):
        named = (routes[0:1, :] == expert) | (routes[1:2, :] == expert)
        codes = jnp.where(named, by_expert[expert], 0.0)
        block = lax.dot_general(
            left,
            codes,
            (((1,), (1,)), ((), ())),
            precision=lax.Precision.HIGHEST,
            preferred_element_type=jnp.float32,
        )
        rows = DOCS_DEV * long
        wide = jnp.concatenate(
            [block[q * rows : (q + 1) * rows] for q in range(group)], axis=1
        )
        for d in range(DOCS_DEV):
            for i in range(long):
                at = d * long + i
                out[d, expert : expert + 1, i * LANES : (i + 1) * LANES] = wide[at : at + 1]


def on_device(tokens, cotangent, routes, doc_ids, gate_weight, up_weight, proj_in, proj_out):
    experts, dats = lax.axis_size("exp"), lax.axis_size("dat")
    home, dat = lax.axis_index("exp"), lax.axis_index("dat")
    core, grp = lax.axis_index("mdl"), lax.axis_index("grp")
    rank, half = proj_in.shape[0], tokens.shape[1]
    swap = [(0, 1), (1, 0)]
    gate, up = gate_weight[0], up_weight[0]

    group = LANES // rank
    reordered = proj_out.reshape(rank // group, group, half).transpose(1, 0, 2)
    grad_mine = lax.dot_general(
        reordered.reshape(rank, half),
        cotangent,
        (((1,), (1,)), ((), ())),
        preferred_element_type=jnp.float32,
    )
    grad_other = lax.ppermute(grad_mine, "mdl", swap)

    unit = half // sum(SPLIT)
    edges = [unit * sum(SPLIT[:j]) for j in range(len(SPLIT) + 1)]
    chunks = list(zip(edges, edges[1:]))
    count = len(chunks)
    ring = [(i, (i + 1) % experts) for i in range(experts)]
    held = [tokens[:, low:high] for low, high in chunks]
    mine, other = [held], [[lax.ppermute(x, "mdl", swap) for x in held]]

    block = gate.shape[0]
    row_edges = [0]
    for share in WAVES:
        row_edges.append(row_edges[-1] + block * share // sum(WAVES) // 16 * 16)
    for at in CUTS:
        row_edges[at] = row_edges[at] // LANES * LANES
    cuts = [row_edges[at] for at in CUTS]
    sent = [
        jnp.where(grp == 0, gate[low:high], up[low:high])
        for low, high in zip(row_edges, row_edges[1:])
    ]
    waves = [[x] for x in sent]

    def along_dat(xs):
        return [
            lax.ppermute(x, "dat", [((z + k) % dats, z) for z in range(dats)])
            for x in xs
            for k in range(1, dats)
        ]

    def over_grp(xs):
        return [lax.ppermute(x, "grp", swap) for x in xs]

    arriving, swapping = along_dat(waves[0]), []
    direct, swapped = [], []

    where = jnp.stack([core, dat, grp]).astype(jnp.int32)

    def joined(part):
        low, high = ((0,) + CUTS)[part : part + 2]
        moves = slice(low * (dats - 1), high * (dats - 1))
        rows = row_edges[low : high + 1]
        return join(where, gate, up, direct[moves], swapped[moves], dats, rows)

    def shards_call(low, high, plan, opened, more, last):
        args = [x for k in range(low, high) for x in (*mine[k], *other[k])]
        used = sorted({part for taken in plan for part in taken})
        rows, shards = tokens.shape[0], high - low
        pieces = 2 * shards * sum(len(segments(*span, cuts)) for span in chunks)
        shape = (rank, rows) if last else (rows, 2 * gate.shape[1])
        return vmem_call(
            functools.partial(shards_kernel, chunks, cuts, plan, opened, last),
            [*args, *[weights[part] for part in used], *more],
            (shards, *shape),
            "shards",
            len(args),
            [
                *[
                    pltpu.VMEM((shards * rows, dats * weights[part].shape[1]), tokens.dtype)
                    for part in used
                ],
                pltpu.SemaphoreType.DMA((pieces,)),
            ],
        )

    turn = jnp.zeros((8, LANES), jnp.float32)
    exchanged, flat, wave, weights, begun = [[], other[0]], [], 0, [], []
    for step in range(1, experts):
        moved = [lax.ppermute(x, "exp", ring) for x in mine[-1]]
        mine.append(moved)
        if step == experts - 1:
            break
        for j in range(count):
            wave += 1
            late = waves[wave] if wave < len(waves) else []
            ready = exchanged.pop(0)
            sizes = [1, len(ready), len(arriving), len(swapping), len(late)]
            turn, got = ordered(turn, [moved[j], *ready, *arriving, *swapping, *late])
            got = [got[sum(sizes[:n]) : sum(sizes[: n + 1])] for n in range(len(sizes))]
            moved[j] = got[0][0]
            flat += got[1]
            direct += got[2]
            swapped += got[3]
            swapping, arriving = over_grp(got[2]), along_dat(got[4])
            exchanged.append([lax.ppermute(moved[j], "mdl", swap)])

    weights.append(joined(0))
    other = [flat[n : n + count] for n in range(0, len(flat), count)]
    groups = [(n, min(n + GROUP, experts - 2)) for n in range(0, experts - 2, GROUP)]
    for low, high in groups:
        begun.append(shards_call(low, high, [(0,)] * (high - low), 0, (), False))
    ready = exchanged.pop(0)
    turn, got = ordered(
        turn, [mine[-1][0], *ready, *swapping], [x[0, :8, :LANES] for x in begun]
    )
    mine[-1][0] = got[0]
    flat += got[1 : 1 + len(ready)] + exchanged.pop(0)
    swapped += got[1 + len(ready) :]
    other = [flat[n : n + count] for n in range(0, len(flat), count)]
    weights.append(joined(1))

    codes = []
    for n, (low, high) in enumerate([*groups, (experts - 2, experts - 1)]):
        if high < experts - 1:
            raw = shards_call(low, high, [(1,)] * (high - low), high - low, (begun[n], proj_in), True)
        else:
            raw = shards_call(low, high, [(0, 1)], 0, (proj_in,), True)
        found = raw + lax.ppermute(raw, "mdl", swap)
        for k in range(low, high):
            back = [(z, (z - k) % experts) for z in range(experts)]
            codes.append(found[0] if k == 0 else lax.ppermute(found[k - low], "exp", back))

    made, total = [grad_other, codes[0], raw[0]], None
    for j in range(count):
        last = j == count - 1
        turn, (x,) = ordered(turn, [mine[-1][j]], made, False) if j else (turn, [mine[-1][j]])
        args = [x, lax.ppermute(x, "mdl", swap), *weights]
        args += [] if total is None else [total]
        args += [proj_in] if last else []
        total = vmem_call(
            functools.partial(part_kernel, chunks[j], cuts, total is None, last),
            args,
            (rank, tokens.shape[0]) if last else (tokens.shape[0], 2 * gate.shape[1]),
            "part",
        )
        made += [total[:8, :LANES]]
    home_pairs = [
        [
            (z * 2 + c, (z + 1) % experts * 2 + (c ^ flip))
            for z in range(experts)
            for c in range(2)
        ]
        for flip in range(2)
    ]
    codes.append(lax.ppermute(total, ("exp", "mdl"), home_pairs[0]))
    cross = lax.ppermute(total, ("exp", "mdl"), home_pairs[1])

    tok_count = tokens.shape[0]
    vmem = pl.BlockSpec(memory_space=pltpu.VMEM)
    return pl.pallas_call(
        functools.partial(grads_kernel, experts),
        in_specs=[pl.BlockSpec(memory_space=pltpu.SMEM)] + [vmem] * (5 + experts),
        out_specs=vmem,
        out_shape=jax.ShapeDtypeStruct((DOCS_DEV, experts, rank * rank), jnp.float32),
        scratch_shapes=[pltpu.VMEM((experts, rank, tok_count), jnp.float32)],
        compiler_params=pltpu.CompilerParams(vmem_limit_bytes=4 * 2**20),
        cost_estimate=pl.CostEstimate(
            flops=2 * experts * DOCS_DEV * rank * rank * tok_count,
            bytes_accessed=2**20,
            transcendentals=0,
        ),
        name="doc_grads",
    )(home.reshape(1), grad_mine, grad_other, doc_ids, routes.T, *codes, cross)


def solution(mesh):
    placed = (
        P(("grp", "exp", "dat"), "mdl"),
        P(("grp", "exp", "dat"), "mdl"),
        P(("grp", "exp", "dat"), None),
        P(("grp", "exp", "dat"), None),
        P("exp", "dat", "mdl"),
        P("exp", "dat", "mdl"),
        P(None, "mdl"),
        P(None, "mdl"),
    )
    return jax.shard_map(
        on_device,
        mesh=mesh,
        in_specs=placed,
        out_specs=P(("grp", "exp", "dat"), None, None),
        check_vma=False,
    )
```

```python
import functools

import jax
import jax.numpy as jnp
from jax import lax
from jax.experimental import pallas as pl
from jax.experimental.pallas import tpu as pltpu
from jax.sharding import PartitionSpec as P

DOCS_DEV = 4
SPLIT = (7, 9)
LANES = 128
GROUP = 3
WAVES = (9, 9, 8, 6)
CUTS = (3, 4)
PIN_BYTES = 24 * 2**20
FREE = pl.CostEstimate(flops=1, bytes_accessed=1, transcendentals=0)


def in_hbm(xs):
    pinned = lax.axis_size("exp") * 2**21 <= PIN_BYTES
    return [pltpu.with_memory_space_constraint(x, pltpu.HBM) if pinned else x for x in xs]


def ordered(turn, arrays, others=(), pin=True):
    hbm = pl.BlockSpec(memory_space=pltpu.HBM)
    kept = [turn, *arrays]
    pin = pin and lax.axis_size("exp") * 2**21 <= PIN_BYTES
    make = pltpu.HBM if pin else jax.ShapeDtypeStruct
    out = pl.pallas_call(
        lambda *refs: None,
        in_specs=[hbm] * len(kept) + [pl.BlockSpec(memory_space=pltpu.VMEM)] * len(others),
        out_specs=[hbm] * len(kept),
        out_shape=[make(x.shape, x.dtype) for x in kept],
        input_output_aliases={i: i for i in range(len(kept))},
        compiler_params=pltpu.CompilerParams(vmem_limit_bytes=2**20),
        name="ordered",
    )(*(in_hbm(kept) if pin else kept), *others)
    return out[0], list(out[1:])


def join_kernel(dats, edges, where, gate, up, *refs):
    pieces = len(edges) - 1
    count = (dats - 1) * pieces
    direct, swapped = refs[:count], refs[count : 2 * count]
    out, sem = refs[2 * count :]
    core, dat, grp = where[0], where[1], where[2]
    cols = gate.shape[1]
    per = dats // 2

    def at(k, i, upper):
        block = lax.rem(dat + k, dats)
        side = jnp.where(lax.div(block, per) == core, 0, 1)
        lanes = pl.ds(pl.multiple_of(upper * cols, LANES), cols)
        rows = pl.ds(edges[i] - edges[0], edges[i + 1] - edges[i])
        return out.at[side * per + lax.rem(block, per), rows, lanes]

    moves = []
    for i in range(pieces):
        rows = pl.ds(edges[i], edges[i + 1] - edges[i])
        moves += [(gate.at[rows], at(0, i, 0)), (up.at[rows], at(0, i, 1))]
        for k in range(1, dats):
            index = i * (dats - 1) + k - 1
            moves += [(direct[index], at(k, i, grp)), (swapped[index], at(k, i, 1 - grp))]
    copies = [pltpu.make_async_copy(a, b, sem.at[i]) for i, (a, b) in enumerate(moves)]
    for copy in copies:
        copy.start()
    for copy in copies:
        copy.wait()


def join(where, gate, up, direct, swapped, dats, edges):
    hbm, vmem = pl.BlockSpec(memory_space=pltpu.HBM), pl.BlockSpec(memory_space=pltpu.VMEM)
    return pl.pallas_call(
        functools.partial(join_kernel, dats, edges),
        in_specs=[pl.BlockSpec(memory_space=pltpu.SMEM)] + [hbm] * (2 + 2 * len(direct)),
        out_specs=vmem,
        out_shape=jax.ShapeDtypeStruct((dats, edges[-1] - edges[0], 2 * gate.shape[1]), gate.dtype),
        scratch_shapes=[pltpu.SemaphoreType.DMA((2 * (len(edges) - 1) * dats,))],
        compiler_params=pltpu.CompilerParams(vmem_limit_bytes=8 * 2**20),
        cost_estimate=FREE,
        name="join",
    )(where, *in_hbm([gate, up, *direct, *swapped]))


def gated(total):
    cols = total.shape[1] // 2
    gate, up = total[:, :cols], total[:, cols:]
    return (gate / (1.0 + jnp.exp(-gate)) * up).astype(jnp.bfloat16)


def segments(low, high, cuts):
    found, at, size = [], low, cuts[-1]
    while at < high:
        start, off = at // size * size, at % size
        part = sum(off >= cut for cut in cuts)
        end = min(high, start + cuts[part])
        found.append((at, end, part, at // size, off - (cuts[part - 1] if part else 0)))
        at = end
    return found


def codes_of(hidden, proj):
    return lax.dot_general(
        proj[...], hidden, (((1,), (1,)), ((), ())), preferred_element_type=jnp.float32
    )


def shards_kernel(spans, cuts, plan, opened, last, *refs):
    count, refs = len(spans), list(refs)
    used = sorted({part for taken in plan for part in taken})
    sources = [refs.pop(0) for _ in range(2 * count * len(plan))]
    weights = {part: refs.pop(0) for part in used}
    sums = refs.pop(0) if opened else None
    proj = refs.pop(0) if last else None
    out, sem = refs.pop(0), refs.pop(-1)
    held = dict(zip(used, refs))
    rows, per = sources[0].shape[0], weights[used[0]].shape[0] // 2

    copies, at = {part: [] for part in used}, 0
    for n, taken in enumerate(plan):
        for i, (low, high) in enumerate(spans):
            for start, end, part, block, row in segments(low, high, cuts):
                for side in range(2) if part in taken else ():
                    place = (side * per + block) * weights[part].shape[1] + row
                    copies[part].append(
                        pltpu.make_async_copy(
                            sources[(2 * n + side) * count + i].at[
                                :, pl.ds(start - low, end - start)
                            ],
                            held[part].at[pl.ds(n * rows, rows), pl.ds(place, end - start)],
                            sem.at[at],
                        )
                    )
                    at += 1
    for part in used:
        for copy in copies[part]:
            copy.start()
    totals = [sums[n] if n < opened else None for n in range(len(plan))]
    for part in used:
        for copy in copies[part]:
            copy.wait()
        takers = [n for n, taken in enumerate(plan) if part in taken]
        mat = weights[part][...]
        mat = mat.reshape(mat.shape[0] * mat.shape[1], mat.shape[2])
        x = held[part][takers[0] * rows : (takers[-1] + 1) * rows]
        found = jnp.dot(x, mat, preferred_element_type=jnp.float32)
        for n in takers:
            own = found[(n - takers[0]) * rows : (n - takers[0] + 1) * rows]
            totals[n] = own if totals[n] is None else totals[n] + own
    for n, total in enumerate(totals):
        out[n] = codes_of(gated(total), proj) if last else total


def part_kernel(span, cuts, first, last, mine, other, *refs):
    weights, refs = refs[: len(cuts)], refs[len(cuts) :]
    per, total = weights[0].shape[0] // 2, None if first else refs[0][...]
    for start, end, part, block, row in segments(*span, cuts):
        for side, x in enumerate((mine, other)):
            piece = jnp.dot(
                x[:, start - span[0] : end - span[0]],
                weights[part][side * per + block, row : row + end - start],
                preferred_element_type=jnp.float32,
            )
            total = piece if total is None else total + piece
    refs[-1][...] = codes_of(gated(total), refs[-2]) if last else total


def vmem_call(kernel, args, shape, name, far=0, scratch=()):
    vmem, hbm = pl.BlockSpec(memory_space=pltpu.VMEM), pl.BlockSpec(memory_space=pltpu.HBM)
    return pl.pallas_call(
        kernel,
        in_specs=[hbm] * far + [vmem] * (len(args) - far),
        out_specs=vmem,
        out_shape=jax.ShapeDtypeStruct(shape, jnp.float32),
        scratch_shapes=scratch,
        compiler_params=pltpu.CompilerParams(vmem_limit_bytes=20 * 2**20),
        cost_estimate=FREE,
        name=name,
    )(*args)


def grads_kernel(steps, experts, where, grad_mine, grad_other, docs, routes, *refs):
    refs = list(refs)
    codes_of_step = [refs.pop(0) for _ in steps]
    cross = refs.pop(0) if experts - 1 in steps else None
    before = refs.pop(0) if cross is not None else None
    out, by_expert = refs
    rank = grad_mine.shape[0]
    group = LANES // rank
    long = rank // group
    home = where[0]
    grad = grad_mine[...] + grad_other[...]
    masks = [docs[...] == d for d in range(DOCS_DEV)]
    left = jnp.concatenate(
        [
            jnp.where(mask, grad[q * long : (q + 1) * long], 0.0)
            for q in range(group)
            for mask in masks
        ],
        axis=0,
    )
    here = [lax.rem(home + k, experts) for k in steps]
    for expert, codes in zip(here, codes_of_step):
        by_expert[expert] = codes[...] if cross is None else codes[...] + cross[...]
    if before is not None:
        out[...] = before[...]
    else:
        by_expert[lax.rem(home + experts - 1, experts)] = jnp.zeros_like(by_expert[0])
    for expert in range(experts) if before is None else here:
        named = (routes[0:1, :] == expert) | (routes[1:2, :] == expert)
        codes = jnp.where(named, by_expert[expert], 0.0)
        block = lax.dot_general(
            left,
            codes,
            (((1,), (1,)), ((), ())),
            precision=lax.Precision.HIGHEST,
            preferred_element_type=jnp.float32,
        )
        rows = DOCS_DEV * long
        wide = jnp.concatenate(
            [block[q * rows : (q + 1) * rows] for q in range(group)], axis=1
        )
        for place in range(experts):
            def store():
                for d in range(DOCS_DEV):
                    for i in range(long):
                        at, lanes = d * long + i, slice(i * LANES, (i + 1) * LANES)
                        out[d, place : place + 1, lanes] = wide[at : at + 1]

            if before is not None:
                pl.when(expert == place)(store)
            elif expert == place:
                store()


def on_device(tokens, cotangent, routes, doc_ids, gate_weight, up_weight, proj_in, proj_out):
    experts, dats = lax.axis_size("exp"), lax.axis_size("dat")
    home, dat = lax.axis_index("exp"), lax.axis_index("dat")
    core, grp = lax.axis_index("mdl"), lax.axis_index("grp")
    rank, half = proj_in.shape[0], tokens.shape[1]
    swap = [(0, 1), (1, 0)]
    gate, up = gate_weight[0], up_weight[0]

    group = LANES // rank
    reordered = proj_out.reshape(rank // group, group, half).transpose(1, 0, 2)
    grad_mine = lax.dot_general(
        reordered.reshape(rank, half),
        cotangent,
        (((1,), (1,)), ((), ())),
        preferred_element_type=jnp.float32,
    )
    grad_other = lax.ppermute(grad_mine, "mdl", swap)

    unit = half // sum(SPLIT)
    edges = [unit * sum(SPLIT[:j]) for j in range(len(SPLIT) + 1)]
    chunks = list(zip(edges, edges[1:]))
    count = len(chunks)
    ring = [(i, (i + 1) % experts) for i in range(experts)]
    held = [tokens[:, low:high] for low, high in chunks]
    mine, other = [held], [[lax.ppermute(x, "mdl", swap) for x in held]]

    block = gate.shape[0]
    row_edges = [0]
    for share in WAVES:
        row_edges.append(row_edges[-1] + block * share // sum(WAVES) // 16 * 16)
    for at in CUTS:
        row_edges[at] = row_edges[at] // LANES * LANES
    cuts = [row_edges[at] for at in CUTS]
    sent = [
        jnp.where(grp == 0, gate[low:high], up[low:high])
        for low, high in zip(row_edges, row_edges[1:])
    ]
    waves = [[x] for x in sent]

    def along_dat(xs):
        return [
            lax.ppermute(x, "dat", [((z + k) % dats, z) for z in range(dats)])
            for x in xs
            for k in range(1, dats)
        ]

    def over_grp(xs):
        return [lax.ppermute(x, "grp", swap) for x in xs]

    arriving, swapping = along_dat(waves[0]), []
    direct, swapped = [], []

    where = jnp.stack([core, dat, grp]).astype(jnp.int32)

    def joined(part):
        low, high = ((0,) + CUTS)[part : part + 2]
        moves = slice(low * (dats - 1), high * (dats - 1))
        rows = row_edges[low : high + 1]
        return join(where, gate, up, direct[moves], swapped[moves], dats, rows)

    def shards_call(low, high, plan, opened, more, last):
        args = [x for k in range(low, high) for x in (*mine[k], *other[k])]
        used = sorted({part for taken in plan for part in taken})
        rows, shards = tokens.shape[0], high - low
        pieces = 2 * shards * sum(len(segments(*span, cuts)) for span in chunks)
        shape = (rank, rows) if last else (rows, 2 * gate.shape[1])
        return vmem_call(
            functools.partial(shards_kernel, chunks, cuts, plan, opened, last),
            [*args, *[weights[part] for part in used], *more],
            (shards, *shape),
            "shards",
            len(args),
            [
                *[
                    pltpu.VMEM((shards * rows, dats * weights[part].shape[1]), tokens.dtype)
                    for part in used
                ],
                pltpu.SemaphoreType.DMA((pieces,)),
            ],
        )

    turn = jnp.zeros((8, LANES), jnp.float32)
    exchanged, flat, wave, weights, begun = [[], other[0]], [], 0, [], []
    for step in range(1, experts):
        moved = [lax.ppermute(x, "exp", ring) for x in mine[-1]]
        mine.append(moved)
        if step == experts - 1:
            break
        for j in range(count):
            wave += 1
            late, others = waves[wave] if wave < len(waves) else [], []
            ready = exchanged.pop(0)
            if wave == 3:
                others = [grad_other]
            sizes = [1, len(ready), len(arriving), len(swapping), len(late)]
            turn, got = ordered(turn, [moved[j], *ready, *arriving, *swapping, *late], others)
            got = [got[sum(sizes[:n]) : sum(sizes[: n + 1])] for n in range(len(sizes))]
            moved[j] = got[0][0]
            flat += got[1]
            direct += got[2]
            swapped += got[3]
            swapping, arriving = over_grp(got[2]), along_dat(got[4])
            exchanged.append([lax.ppermute(moved[j], "mdl", swap)])

    weights.append(joined(0))
    other = [flat[n : n + count] for n in range(0, len(flat), count)]
    groups = [(n, min(n + GROUP, experts - 2)) for n in range(0, experts - 2, GROUP)]
    for low, high in groups:
        begun.append(shards_call(low, high, [(0,)] * (high - low), 0, (), False))
    ready = exchanged.pop(0)
    turn, got = ordered(
        turn, [mine[-1][0], *ready, *swapping], [x[0, :8, :LANES] for x in begun]
    )
    mine[-1][0] = got[0]
    flat += got[1 : 1 + len(ready)] + exchanged.pop(0)
    swapped += got[1 + len(ready) :]
    other = [flat[n : n + count] for n in range(0, len(flat), count)]
    weights.append(joined(1))

    codes = []
    for n, (low, high) in enumerate([*groups, (experts - 2, experts - 1)]):
        if high < experts - 1:
            raw = shards_call(low, high, [(1,)] * (high - low), high - low, (begun[n], proj_in), True)
        else:
            raw = shards_call(low, high, [(0, 1)], 0, (proj_in,), True)
        found = raw + lax.ppermute(raw, "mdl", swap)
        for k in range(low, high):
            back = [(z, (z - k) % experts) for z in range(experts)]
            codes.append(found[0] if k == 0 else lax.ppermute(found[k - low], "exp", back))

    made, total = [codes[0], raw[0]], None
    for j in range(count):
        last = j == count - 1
        turn, (x,) = ordered(turn, [mine[-1][j]], made, False) if j else (turn, [mine[-1][j]])
        args = [x, lax.ppermute(x, "mdl", swap), *weights]
        args += [] if total is None else [total]
        args += [proj_in] if last else []
        total = vmem_call(
            functools.partial(part_kernel, chunks[j], cuts, total is None, last),
            args,
            (rank, tokens.shape[0]) if last else (tokens.shape[0], 2 * gate.shape[1]),
            "part",
        )
    home_pairs = [
        [
            (z * 2 + c, (z + 1) % experts * 2 + (c ^ flip))
            for z in range(experts)
            for c in range(2)
        ]
        for flip in range(2)
    ]
    codes.append(lax.ppermute(total, ("exp", "mdl"), home_pairs[0]))
    cross = lax.ppermute(total, ("exp", "mdl"), home_pairs[1])

    def grads(steps, more):
        vmem = pl.BlockSpec(memory_space=pltpu.VMEM)
        args = [grad_mine, grad_other, doc_ids, routes.T, *[codes[k] for k in steps], *more]
        return pl.pallas_call(
            functools.partial(grads_kernel, steps, experts),
            in_specs=[pl.BlockSpec(memory_space=pltpu.SMEM)] + [vmem] * len(args),
            out_specs=vmem,
            out_shape=jax.ShapeDtypeStruct((DOCS_DEV, experts, rank * rank), jnp.float32),
            scratch_shapes=[pltpu.VMEM((experts, rank, tokens.shape[0]), jnp.float32)],
            compiler_params=pltpu.CompilerParams(vmem_limit_bytes=4 * 2**20),
            cost_estimate=FREE,
            name="doc_grads",
        )(home.reshape(1), *args)

    first = grads(range(experts - 1), ())
    return grads(range(experts - 1, experts), (cross, first))


def solution(mesh):
    placed = (
        P(("grp", "exp", "dat"), "mdl"),
        P(("grp", "exp", "dat"), "mdl"),
        P(("grp", "exp", "dat"), None),
        P(("grp", "exp", "dat"), None),
        P("exp", "dat", "mdl"),
        P("exp", "dat", "mdl"),
        P(None, "mdl"),
        P(None, "mdl"),
    )
    return jax.shard_map(
        on_device,
        mesh=mesh,
        in_specs=placed,
        out_specs=P(("grp", "exp", "dat"), None, None),
        check_vma=False,
    )
```

```python
import functools

import jax
import jax.numpy as jnp
from jax import lax
from jax.experimental import pallas as pl
from jax.experimental.pallas import tpu as pltpu
from jax.sharding import PartitionSpec as P

DOCS_DEV = 4
SPLIT = (7, 9)
LANES = 128
GROUP = 3
WAVES = (9, 9, 8, 6)
CUTS = (3, 4)
PIN_BYTES = 24 * 2**20
FREE = pl.CostEstimate(flops=1, bytes_accessed=1, transcendentals=0)


def in_hbm(xs):
    pinned = lax.axis_size("exp") * 2**21 <= PIN_BYTES
    return [pltpu.with_memory_space_constraint(x, pltpu.HBM) if pinned else x for x in xs]


def ordered(turn, arrays, others=(), pin=True):
    hbm = pl.BlockSpec(memory_space=pltpu.HBM)
    kept = [turn, *arrays]
    pin = pin and lax.axis_size("exp") * 2**21 <= PIN_BYTES
    make = pltpu.HBM if pin else jax.ShapeDtypeStruct
    out = pl.pallas_call(
        lambda *refs: None,
        in_specs=[hbm] * len(kept) + [pl.BlockSpec(memory_space=pltpu.VMEM)] * len(others),
        out_specs=[hbm] * len(kept),
        out_shape=[make(x.shape, x.dtype) for x in kept],
        input_output_aliases={i: i for i in range(len(kept))},
        compiler_params=pltpu.CompilerParams(vmem_limit_bytes=2**20),
        name="ordered",
    )(*(in_hbm(kept) if pin else kept), *others)
    return out[0], list(out[1:])


def join_kernel(dats, edges, where, gate, up, *refs):
    pieces = len(edges) - 1
    count = (dats - 1) * pieces
    direct, swapped = refs[:count], refs[count : 2 * count]
    out, sem = refs[2 * count :]
    core, dat, grp = where[0], where[1], where[2]
    cols = gate.shape[1]
    per = dats // 2

    def at(k, i, upper):
        block = lax.rem(dat + k, dats)
        side = jnp.where(lax.div(block, per) == core, 0, 1)
        lanes = pl.ds(pl.multiple_of(upper * cols, LANES), cols)
        rows = pl.ds(edges[i] - edges[0], edges[i + 1] - edges[i])
        return out.at[side * per + lax.rem(block, per), rows, lanes]

    moves = []
    for i in range(pieces):
        rows = pl.ds(edges[i], edges[i + 1] - edges[i])
        moves += [(gate.at[rows], at(0, i, 0)), (up.at[rows], at(0, i, 1))]
        for k in range(1, dats):
            index = i * (dats - 1) + k - 1
            moves += [(direct[index], at(k, i, grp)), (swapped[index], at(k, i, 1 - grp))]
    copies = [pltpu.make_async_copy(a, b, sem.at[i]) for i, (a, b) in enumerate(moves)]
    for copy in copies:
        copy.start()
    for copy in copies:
        copy.wait()


def join(where, gate, up, direct, swapped, dats, edges):
    hbm, vmem = pl.BlockSpec(memory_space=pltpu.HBM), pl.BlockSpec(memory_space=pltpu.VMEM)
    return pl.pallas_call(
        functools.partial(join_kernel, dats, edges),
        in_specs=[pl.BlockSpec(memory_space=pltpu.SMEM)] + [hbm] * (2 + 2 * len(direct)),
        out_specs=vmem,
        out_shape=jax.ShapeDtypeStruct((dats, edges[-1] - edges[0], 2 * gate.shape[1]), gate.dtype),
        scratch_shapes=[pltpu.SemaphoreType.DMA((2 * (len(edges) - 1) * dats,))],
        compiler_params=pltpu.CompilerParams(vmem_limit_bytes=8 * 2**20),
        cost_estimate=FREE,
        name="join",
    )(where, *in_hbm([gate, up, *direct, *swapped]))


def gated(total):
    cols = total.shape[1] // 2
    gate, up = total[:, :cols], total[:, cols:]
    return (gate / (1.0 + jnp.exp(-gate)) * up).astype(jnp.bfloat16)


def segments(low, high, cuts):
    found, at, size = [], low, cuts[-1]
    while at < high:
        start, off = at // size * size, at % size
        part = sum(off >= cut for cut in cuts)
        end = min(high, start + cuts[part])
        found.append((at, end, part, at // size, off - (cuts[part - 1] if part else 0)))
        at = end
    return found


def codes_of(hidden, proj):
    return lax.dot_general(
        proj[...], hidden, (((1,), (1,)), ((), ())), preferred_element_type=jnp.float32
    )


def shards_kernel(spans, cuts, plan, opened, last, *refs):
    count, refs = len(spans), list(refs)
    used = sorted({part for taken in plan for part in taken})
    sources = [refs.pop(0) for _ in range(2 * count * len(plan))]
    weights = {part: refs.pop(0) for part in used}
    sums = refs.pop(0) if opened else None
    proj = refs.pop(0) if last else None
    out, sem = refs.pop(0), refs.pop(-1)
    held = dict(zip(used, refs))
    rows, per = sources[0].shape[0], weights[used[0]].shape[0] // 2

    copies, at = {part: [] for part in used}, 0
    for n, taken in enumerate(plan):
        for i, (low, high) in enumerate(spans):
            for start, end, part, block, row in segments(low, high, cuts):
                for side in range(2) if part in taken else ():
                    place = (side * per + block) * weights[part].shape[1] + row
                    copies[part].append(
                        pltpu.make_async_copy(
                            sources[(2 * n + side) * count + i].at[
                                :, pl.ds(start - low, end - start)
                            ],
                            held[part].at[pl.ds(n * rows, rows), pl.ds(place, end - start)],
                            sem.at[at],
                        )
                    )
                    at += 1
    for part in used:
        for copy in copies[part]:
            copy.start()
    totals = [sums[n] if n < opened else None for n in range(len(plan))]
    for part in used:
        for copy in copies[part]:
            copy.wait()
        takers = [n for n, taken in enumerate(plan) if part in taken]
        mat = weights[part][...]
        mat = mat.reshape(mat.shape[0] * mat.shape[1], mat.shape[2])
        x = held[part][takers[0] * rows : (takers[-1] + 1) * rows]
        found = jnp.dot(x, mat, preferred_element_type=jnp.float32)
        for n in takers:
            own = found[(n - takers[0]) * rows : (n - takers[0] + 1) * rows]
            totals[n] = own if totals[n] is None else totals[n] + own
    for n, total in enumerate(totals):
        out[n] = codes_of(gated(total), proj) if last else total


def part_kernel(span, cuts, first, last, mine, other, *refs):
    weights, refs = refs[: len(cuts)], refs[len(cuts) :]
    per, total = weights[0].shape[0] // 2, None if first else refs[0][...]
    for start, end, part, block, row in segments(*span, cuts):
        for side, x in enumerate((mine, other)):
            piece = jnp.dot(
                x[:, start - span[0] : end - span[0]],
                weights[part][side * per + block, row : row + end - start],
                preferred_element_type=jnp.float32,
            )
            total = piece if total is None else total + piece
    refs[-1][...] = codes_of(gated(total), refs[-2]) if last else total


def vmem_call(kernel, args, shape, name, far=0, scratch=()):
    vmem, hbm = pl.BlockSpec(memory_space=pltpu.VMEM), pl.BlockSpec(memory_space=pltpu.HBM)
    return pl.pallas_call(
        kernel,
        in_specs=[hbm] * far + [vmem] * (len(args) - far),
        out_specs=vmem,
        out_shape=jax.ShapeDtypeStruct(shape, jnp.float32),
        scratch_shapes=scratch,
        compiler_params=pltpu.CompilerParams(vmem_limit_bytes=20 * 2**20),
        cost_estimate=FREE,
        name=name,
    )(*args)


def grads_kernel(steps, experts, where, grad_mine, grad_other, docs, routes, *refs):
    refs = list(refs)
    codes_of_step = [refs.pop(0) for _ in steps]
    before = refs.pop(0) if experts - 1 in steps else None
    out, by_expert = refs
    rank = grad_mine.shape[0]
    group = LANES // rank
    long = rank // group
    home = where[0]
    grad = grad_mine[...] + grad_other[...]
    masks = [docs[...] == d for d in range(DOCS_DEV)]
    left = jnp.concatenate(
        [
            jnp.where(mask, grad[q * long : (q + 1) * long], 0.0)
            for q in range(group)
            for mask in masks
        ],
        axis=0,
    )
    here = [lax.rem(home + k, experts) for k in steps]
    for expert, codes in zip(here, codes_of_step):
        by_expert[expert] = codes[...]
    if before is not None:
        out[...] = before[...]
    else:
        by_expert[lax.rem(home + experts - 1, experts)] = jnp.zeros_like(by_expert[0])
    for expert in range(experts) if before is None else here:
        named = (routes[0:1, :] == expert) | (routes[1:2, :] == expert)
        codes = jnp.where(named, by_expert[expert], 0.0)
        block = lax.dot_general(
            left,
            codes,
            (((1,), (1,)), ((), ())),
            precision=lax.Precision.HIGHEST,
            preferred_element_type=jnp.float32,
        )
        rows = DOCS_DEV * long
        wide = jnp.concatenate(
            [block[q * rows : (q + 1) * rows] for q in range(group)], axis=1
        )
        for place in range(experts):
            def store():
                for d in range(DOCS_DEV):
                    for i in range(long):
                        at, lanes = d * long + i, slice(i * LANES, (i + 1) * LANES)
                        out[d, place : place + 1, lanes] = wide[at : at + 1]

            if before is not None:
                pl.when(expert == place)(store)
            elif expert == place:
                store()


def on_device(tokens, cotangent, routes, doc_ids, gate_weight, up_weight, proj_in, proj_out):
    experts, dats = lax.axis_size("exp"), lax.axis_size("dat")
    home, dat = lax.axis_index("exp"), lax.axis_index("dat")
    core, grp = lax.axis_index("mdl"), lax.axis_index("grp")
    rank, half = proj_in.shape[0], tokens.shape[1]
    swap = [(0, 1), (1, 0)]
    gate, up = gate_weight[0], up_weight[0]

    group = LANES // rank
    reordered = proj_out.reshape(rank // group, group, half).transpose(1, 0, 2)
    grad_mine = lax.dot_general(
        reordered.reshape(rank, half),
        cotangent,
        (((1,), (1,)), ((), ())),
        preferred_element_type=jnp.float32,
    )
    grad_other = lax.ppermute(grad_mine, "mdl", swap)

    unit = half // sum(SPLIT)
    edges = [unit * sum(SPLIT[:j]) for j in range(len(SPLIT) + 1)]
    chunks = list(zip(edges, edges[1:]))
    count = len(chunks)
    ring = [(i, (i + 1) % experts) for i in range(experts)]
    held = [tokens[:, low:high] for low, high in chunks]
    mine, other = [held], [[lax.ppermute(x, "mdl", swap) for x in held]]

    block = gate.shape[0]
    row_edges = [0]
    for share in WAVES:
        row_edges.append(row_edges[-1] + block * share // sum(WAVES) // 16 * 16)
    for at in CUTS:
        row_edges[at] = row_edges[at] // LANES * LANES
    cuts = [row_edges[at] for at in CUTS]
    sent = [
        jnp.where(grp == 0, gate[low:high], up[low:high])
        for low, high in zip(row_edges, row_edges[1:])
    ]
    waves = [[x] for x in sent]

    def along_dat(xs):
        return [
            lax.ppermute(x, "dat", [((z + k) % dats, z) for z in range(dats)])
            for x in xs
            for k in range(1, dats)
        ]

    def over_grp(xs):
        return [lax.ppermute(x, "grp", swap) for x in xs]

    arriving, swapping = along_dat(waves[0]), []
    direct, swapped = [], []

    where = jnp.stack([core, dat, grp]).astype(jnp.int32)

    def joined(part):
        low, high = ((0,) + CUTS)[part : part + 2]
        moves = slice(low * (dats - 1), high * (dats - 1))
        rows = row_edges[low : high + 1]
        return join(where, gate, up, direct[moves], swapped[moves], dats, rows)

    def shards_call(low, high, plan, opened, more, last):
        args = [x for k in range(low, high) for x in (*mine[k], *other[k])]
        used = sorted({part for taken in plan for part in taken})
        rows, shards = tokens.shape[0], high - low
        pieces = 2 * shards * sum(len(segments(*span, cuts)) for span in chunks)
        shape = (rank, rows) if last else (rows, 2 * gate.shape[1])
        return vmem_call(
            functools.partial(shards_kernel, chunks, cuts, plan, opened, last),
            [*args, *[weights[part] for part in used], *more],
            (shards, *shape),
            "shards",
            len(args),
            [
                *[
                    pltpu.VMEM((shards * rows, dats * weights[part].shape[1]), tokens.dtype)
                    for part in used
                ],
                pltpu.SemaphoreType.DMA((pieces,)),
            ],
        )

    turn = jnp.zeros((8, LANES), jnp.float32)
    exchanged, flat, wave, weights, begun = [[], other[0]], [], 0, [], []
    for step in range(1, experts):
        moved = [lax.ppermute(x, "exp", ring) for x in mine[-1]]
        mine.append(moved)
        if step == experts - 1:
            break
        for j in range(count):
            wave += 1
            late, others = waves[wave] if wave < len(waves) else [], []
            ready = exchanged.pop(0)
            if wave == 3:
                others = [grad_other]
            sizes = [1, len(ready), len(arriving), len(swapping), len(late)]
            turn, got = ordered(turn, [moved[j], *ready, *arriving, *swapping, *late], others)
            got = [got[sum(sizes[:n]) : sum(sizes[: n + 1])] for n in range(len(sizes))]
            moved[j] = got[0][0]
            flat += got[1]
            direct += got[2]
            swapped += got[3]
            swapping, arriving = over_grp(got[2]), along_dat(got[4])
            exchanged.append([lax.ppermute(moved[j], "mdl", swap)])

    weights.append(joined(0))
    other = [flat[n : n + count] for n in range(0, len(flat), count)]
    groups = [(n, min(n + GROUP, experts - 2)) for n in range(0, experts - 2, GROUP)]
    for low, high in groups:
        begun.append(shards_call(low, high, [(0,)] * (high - low), 0, (), False))
    ready = exchanged.pop(0)
    turn, got = ordered(
        turn, [mine[-1][0], *ready, *swapping], [x[0, :8, :LANES] for x in begun]
    )
    mine[-1][0] = got[0]
    flat += got[1 : 1 + len(ready)] + exchanged.pop(0)
    swapped += got[1 + len(ready) :]
    other = [flat[n : n + count] for n in range(0, len(flat), count)]
    weights.append(joined(1))

    codes = []
    for n, (low, high) in enumerate([*groups, (experts - 2, experts - 1)]):
        if high < experts - 1:
            raw = shards_call(low, high, [(1,)] * (high - low), high - low, (begun[n], proj_in), True)
        else:
            raw = shards_call(low, high, [(0, 1)], 0, (proj_in,), True)
        found = raw + lax.ppermute(raw, "mdl", swap)
        for k in range(low, high):
            back = [(z, (z - k) % experts) for z in range(experts)]
            codes.append(found[0] if k == 0 else lax.ppermute(found[k - low], "exp", back))

    made, total = [codes[0], raw[0]], None
    for j in range(count):
        last = j == count - 1
        turn, (x,) = ordered(turn, [mine[-1][j]], made, False) if j else (turn, [mine[-1][j]])
        args = [x, lax.ppermute(x, "mdl", swap), *weights]
        args += [] if total is None else [total]
        args += [proj_in] if last else []
        total = vmem_call(
            functools.partial(part_kernel, chunks[j], cuts, total is None, last),
            args,
            (rank, tokens.shape[0]) if last else (tokens.shape[0], 2 * gate.shape[1]),
            "part",
        )
    total = total + lax.ppermute(total, "mdl", swap)
    codes.append(lax.ppermute(total, "exp", ring))

    def grads(steps, more):
        vmem = pl.BlockSpec(memory_space=pltpu.VMEM)
        args = [grad_mine, grad_other, doc_ids, routes.T, *[codes[k] for k in steps], *more]
        return pl.pallas_call(
            functools.partial(grads_kernel, steps, experts),
            in_specs=[pl.BlockSpec(memory_space=pltpu.SMEM)] + [vmem] * len(args),
            out_specs=vmem,
            out_shape=jax.ShapeDtypeStruct((DOCS_DEV, experts, rank * rank), jnp.float32),
            scratch_shapes=[pltpu.VMEM((experts, rank, tokens.shape[0]), jnp.float32)],
            compiler_params=pltpu.CompilerParams(vmem_limit_bytes=4 * 2**20),
            cost_estimate=FREE,
            name="doc_grads",
        )(home.reshape(1), *args)

    first = grads(range(experts - 1), ())
    return grads(range(experts - 1, experts), (first,))


def solution(mesh):
    placed = (
        P(("grp", "exp", "dat"), "mdl"),
        P(("grp", "exp", "dat"), "mdl"),
        P(("grp", "exp", "dat"), None),
        P(("grp", "exp", "dat"), None),
        P("exp", "dat", "mdl"),
        P("exp", "dat", "mdl"),
        P(None, "mdl"),
        P(None, "mdl"),
    )
    return jax.shard_map(
        on_device,
        mesh=mesh,
        in_specs=placed,
        out_specs=P(("grp", "exp", "dat"), None, None),
        check_vma=False,
    )
```

```python
import functools

import jax
import jax.numpy as jnp
from jax import lax
from jax.experimental import pallas as pl
from jax.experimental.pallas import tpu as pltpu
from jax.sharding import PartitionSpec as P

DOCS_DEV = 4
SPLIT = (7, 9)
LANES = 128
GROUP = 3
WAVES = (9, 9, 8, 6)
CUTS = (3, 4)
PIN_BYTES = 24 * 2**20
FREE = pl.CostEstimate(flops=1, bytes_accessed=1, transcendentals=0)


def in_hbm(xs):
    pinned = lax.axis_size("exp") * 2**21 <= PIN_BYTES
    return [pltpu.with_memory_space_constraint(x, pltpu.HBM) if pinned else x for x in xs]


def ordered(turn, arrays, others=(), pin=True):
    hbm = pl.BlockSpec(memory_space=pltpu.HBM)
    kept = [turn, *arrays]
    pin = pin and lax.axis_size("exp") * 2**21 <= PIN_BYTES
    make = pltpu.HBM if pin else jax.ShapeDtypeStruct
    out = pl.pallas_call(
        lambda *refs: None,
        in_specs=[hbm] * len(kept) + [pl.BlockSpec(memory_space=pltpu.VMEM)] * len(others),
        out_specs=[hbm] * len(kept),
        out_shape=[make(x.shape, x.dtype) for x in kept],
        input_output_aliases={i: i for i in range(len(kept))},
        compiler_params=pltpu.CompilerParams(vmem_limit_bytes=2**20),
        name="ordered",
    )(*(in_hbm(kept) if pin else kept), *others)
    return out[0], list(out[1:])


def join_kernel(dats, edges, where, gate, up, *refs):
    pieces = len(edges) - 1
    count = (dats - 1) * pieces
    direct, swapped = refs[:count], refs[count : 2 * count]
    out, sem = refs[2 * count :]
    core, dat, grp = where[0], where[1], where[2]
    cols = gate.shape[1]
    per = dats // 2

    def at(k, i, upper):
        block = lax.rem(dat + k, dats)
        side = jnp.where(lax.div(block, per) == core, 0, 1)
        lanes = pl.ds(pl.multiple_of(upper * cols, LANES), cols)
        rows = pl.ds(edges[i] - edges[0], edges[i + 1] - edges[i])
        return out.at[side * per + lax.rem(block, per), rows, lanes]

    moves = []
    for i in range(pieces):
        rows = pl.ds(edges[i], edges[i + 1] - edges[i])
        moves += [(gate.at[rows], at(0, i, 0)), (up.at[rows], at(0, i, 1))]
        for k in range(1, dats):
            index = i * (dats - 1) + k - 1
            moves += [(direct[index], at(k, i, grp)), (swapped[index], at(k, i, 1 - grp))]
    copies = [pltpu.make_async_copy(a, b, sem.at[i]) for i, (a, b) in enumerate(moves)]
    for copy in copies:
        copy.start()
    for copy in copies:
        copy.wait()


def join(where, gate, up, direct, swapped, dats, edges):
    hbm, vmem = pl.BlockSpec(memory_space=pltpu.HBM), pl.BlockSpec(memory_space=pltpu.VMEM)
    return pl.pallas_call(
        functools.partial(join_kernel, dats, edges),
        in_specs=[pl.BlockSpec(memory_space=pltpu.SMEM)] + [hbm] * (2 + 2 * len(direct)),
        out_specs=vmem,
        out_shape=jax.ShapeDtypeStruct((dats, edges[-1] - edges[0], 2 * gate.shape[1]), gate.dtype),
        scratch_shapes=[pltpu.SemaphoreType.DMA((2 * (len(edges) - 1) * dats,))],
        compiler_params=pltpu.CompilerParams(vmem_limit_bytes=8 * 2**20),
        cost_estimate=FREE,
        name="join",
    )(where, *in_hbm([gate, up, *direct, *swapped]))


def gated(total):
    cols = total.shape[1] // 2
    gate, up = total[:, :cols], total[:, cols:]
    return (gate / (1.0 + jnp.exp(-gate)) * up).astype(jnp.bfloat16)


def segments(low, high, cuts):
    found, at, size = [], low, cuts[-1]
    while at < high:
        start, off = at // size * size, at % size
        part = sum(off >= cut for cut in cuts)
        end = min(high, start + cuts[part])
        found.append((at, end, part, at // size, off - (cuts[part - 1] if part else 0)))
        at = end
    return found


def codes_of(hidden, proj):
    return lax.dot_general(
        proj[...], hidden, (((1,), (1,)), ((), ())), preferred_element_type=jnp.float32
    )


def shards_kernel(spans, cuts, plan, opened, last, *refs):
    count, refs = len(spans), list(refs)
    used = sorted({part for taken in plan for part in taken})
    sources = [refs.pop(0) for _ in range(2 * count * len(plan))]
    weights = {part: refs.pop(0) for part in used}
    sums = refs.pop(0) if opened else None
    proj = refs.pop(0) if last else None
    out, sem = refs.pop(0), refs.pop(-1)
    held = dict(zip(used, refs))
    rows, per = sources[0].shape[0], weights[used[0]].shape[0] // 2

    copies, at = {part: [] for part in used}, 0
    for n, taken in enumerate(plan):
        for i, (low, high) in enumerate(spans):
            for start, end, part, block, row in segments(low, high, cuts):
                for side in range(2) if part in taken else ():
                    place = (side * per + block) * weights[part].shape[1] + row
                    copies[part].append(
                        pltpu.make_async_copy(
                            sources[(2 * n + side) * count + i].at[
                                :, pl.ds(start - low, end - start)
                            ],
                            held[part].at[pl.ds(n * rows, rows), pl.ds(place, end - start)],
                            sem.at[at],
                        )
                    )
                    at += 1
    for part in used:
        for copy in copies[part]:
            copy.start()
    totals = [sums[n] if n < opened else None for n in range(len(plan))]
    for part in used:
        for copy in copies[part]:
            copy.wait()
        takers = [n for n, taken in enumerate(plan) if part in taken]
        mat = weights[part][...]
        mat = mat.reshape(mat.shape[0] * mat.shape[1], mat.shape[2])
        x = held[part][takers[0] * rows : (takers[-1] + 1) * rows]
        found = jnp.dot(x, mat, preferred_element_type=jnp.float32)
        for n in takers:
            own = found[(n - takers[0]) * rows : (n - takers[0] + 1) * rows]
            totals[n] = own if totals[n] is None else totals[n] + own
    for n, total in enumerate(totals):
        out[n] = codes_of(gated(total), proj) if last else total


def part_kernel(span, cuts, first, last, mine, other, *refs):
    weights, refs = refs[: len(cuts)], refs[len(cuts) :]
    per, total = weights[0].shape[0] // 2, None if first else refs[0][...]
    for start, end, part, block, row in segments(*span, cuts):
        for side, x in enumerate((mine, other)):
            piece = jnp.dot(
                x[:, start - span[0] : end - span[0]],
                weights[part][side * per + block, row : row + end - start],
                preferred_element_type=jnp.float32,
            )
            total = piece if total is None else total + piece
    refs[-1][...] = codes_of(gated(total), refs[-2]) if last else total


def vmem_call(kernel, args, shape, name, far=0, scratch=()):
    vmem, hbm = pl.BlockSpec(memory_space=pltpu.VMEM), pl.BlockSpec(memory_space=pltpu.HBM)
    return pl.pallas_call(
        kernel,
        in_specs=[hbm] * far + [vmem] * (len(args) - far),
        out_specs=vmem,
        out_shape=jax.ShapeDtypeStruct(shape, jnp.float32),
        scratch_shapes=scratch,
        compiler_params=pltpu.CompilerParams(vmem_limit_bytes=20 * 2**20),
        cost_estimate=FREE,
        name=name,
    )(*args)


def grads_kernel(steps, experts, where, grad_mine, grad_other, docs, routes, *refs):
    refs = list(refs)
    codes_of_step = [refs.pop(0) for _ in steps]
    before = refs.pop(0) if experts - 1 in steps else None
    out, by_expert = refs
    rank = grad_mine.shape[0]
    group = LANES // rank
    long = rank // group
    home = where[0]
    grad = grad_mine[...] + grad_other[...]
    masks = [docs[...] == d for d in range(DOCS_DEV)]
    left = jnp.concatenate(
        [
            jnp.where(mask, grad[q * long : (q + 1) * long], 0.0)
            for q in range(group)
            for mask in masks
        ],
        axis=0,
    )
    here = [lax.rem(home + k, experts) for k in steps]
    for expert, codes in zip(here, codes_of_step):
        by_expert[expert] = codes[...]
    if before is not None:
        out[...] = before[...]
    else:
        by_expert[lax.rem(home + experts - 1, experts)] = jnp.zeros_like(by_expert[0])
    for expert in range(experts) if before is None else here:
        named = (routes[0:1, :] == expert) | (routes[1:2, :] == expert)
        codes = jnp.where(named, by_expert[expert], 0.0)
        block = lax.dot_general(
            left,
            codes,
            (((1,), (1,)), ((), ())),
            precision=lax.Precision.HIGHEST,
            preferred_element_type=jnp.float32,
        )
        rows = DOCS_DEV * long
        wide = jnp.concatenate(
            [block[q * rows : (q + 1) * rows] for q in range(group)], axis=1
        )
        for place in range(experts):
            def store():
                for d in range(DOCS_DEV):
                    for i in range(long):
                        at, lanes = d * long + i, slice(i * LANES, (i + 1) * LANES)
                        out[d, place : place + 1, lanes] = wide[at : at + 1]

            if before is not None:
                pl.when(expert == place)(store)
            elif expert == place:
                store()


def on_device(tokens, cotangent, routes, doc_ids, gate_weight, up_weight, proj_in, proj_out):
    experts, dats = lax.axis_size("exp"), lax.axis_size("dat")
    home, dat = lax.axis_index("exp"), lax.axis_index("dat")
    core, grp = lax.axis_index("mdl"), lax.axis_index("grp")
    rank, half = proj_in.shape[0], tokens.shape[1]
    swap = [(0, 1), (1, 0)]
    gate, up = gate_weight[0], up_weight[0]

    group = LANES // rank
    reordered = proj_out.reshape(rank // group, group, half).transpose(1, 0, 2)
    grad_mine = lax.dot_general(
        reordered.reshape(rank, half),
        cotangent,
        (((1,), (1,)), ((), ())),
        preferred_element_type=jnp.float32,
    )
    grad_other = lax.ppermute(grad_mine, "mdl", swap)

    unit = half // sum(SPLIT)
    edges = [unit * sum(SPLIT[:j]) for j in range(len(SPLIT) + 1)]
    chunks = list(zip(edges, edges[1:]))
    count = len(chunks)
    ring = [(i, (i + 1) % experts) for i in range(experts)]
    held = [tokens[:, low:high] for low, high in chunks]
    mine, other = [held], [[lax.ppermute(x, "mdl", swap) for x in held]]

    block = gate.shape[0]
    row_edges = [0]
    for share in WAVES:
        row_edges.append(row_edges[-1] + block * share // sum(WAVES) // 16 * 16)
    for at in CUTS:
        row_edges[at] = row_edges[at] // LANES * LANES
    cuts = [row_edges[at] for at in CUTS]
    sent = [
        jnp.where(grp == 0, gate[low:high], up[low:high])
        for low, high in zip(row_edges, row_edges[1:])
    ]
    waves = [[x] for x in sent]

    def along_dat(xs):
        return [
            lax.ppermute(x, "dat", [((z + k) % dats, z) for z in range(dats)])
            for x in xs
            for k in range(1, dats)
        ]

    def over_grp(xs):
        return [lax.ppermute(x, "grp", swap) for x in xs]

    arriving, swapping = along_dat(waves[0]), []
    direct, swapped = [], []

    where = jnp.stack([core, dat, grp]).astype(jnp.int32)

    def joined(part):
        low, high = ((0,) + CUTS)[part : part + 2]
        moves = slice(low * (dats - 1), high * (dats - 1))
        rows = row_edges[low : high + 1]
        return join(where, gate, up, direct[moves], swapped[moves], dats, rows)

    def shards_call(low, high, plan, opened, more, last):
        args = [x for k in range(low, high) for x in (*mine[k], *other[k])]
        used = sorted({part for taken in plan for part in taken})
        rows, shards = tokens.shape[0], high - low
        pieces = 2 * shards * sum(len(segments(*span, cuts)) for span in chunks)
        shape = (rank, rows) if last else (rows, 2 * gate.shape[1])
        return vmem_call(
            functools.partial(shards_kernel, chunks, cuts, plan, opened, last),
            [*args, *[weights[part] for part in used], *more],
            (shards, *shape),
            "shards",
            len(args),
            [
                *[
                    pltpu.VMEM((shards * rows, dats * weights[part].shape[1]), tokens.dtype)
                    for part in used
                ],
                pltpu.SemaphoreType.DMA((pieces,)),
            ],
        )

    turn = jnp.zeros((8, LANES), jnp.float32)
    exchanged, flat, wave, weights, begun = [[], other[0]], [], 0, [], []
    for step in range(1, experts):
        moved = [lax.ppermute(x, "exp", ring) for x in mine[-1]]
        mine.append(moved)
        if step == experts - 1:
            break
        for j in range(count):
            wave += 1
            late, others = waves[wave] if wave < len(waves) else [], []
            ready = exchanged.pop(0)
            if wave == 3:
                others = [grad_other]
            sizes = [1, len(ready), len(arriving), len(swapping), len(late)]
            turn, got = ordered(turn, [moved[j], *ready, *arriving, *swapping, *late], others)
            got = [got[sum(sizes[:n]) : sum(sizes[: n + 1])] for n in range(len(sizes))]
            moved[j] = got[0][0]
            flat += got[1]
            direct += got[2]
            swapped += got[3]
            swapping, arriving = over_grp(got[2]), along_dat(got[4])
            exchanged.append([lax.ppermute(moved[j], "mdl", swap)])

    weights.append(joined(0))
    other = [flat[n : n + count] for n in range(0, len(flat), count)]
    groups = [(n, min(n + GROUP, experts - 2)) for n in range(0, experts - 2, GROUP)]
    for low, high in groups:
        begun.append(shards_call(low, high, [(0,)] * (high - low), 0, (), False))
    ready = exchanged.pop(0)
    turn, got = ordered(
        turn, [mine[-1][0], *ready, *swapping], [x[0, :8, :LANES] for x in begun], False
    )
    mine[-1][0] = got[0]
    flat += got[1 : 1 + len(ready)] + exchanged.pop(0)
    swapped += got[1 + len(ready) :]
    other = [flat[n : n + count] for n in range(0, len(flat), count)]
    weights.append(joined(1))

    codes = []
    for n, (low, high) in enumerate([*groups, (experts - 2, experts - 1)]):
        if high < experts - 1:
            raw = shards_call(low, high, [(1,)] * (high - low), high - low, (begun[n], proj_in), True)
        else:
            raw = shards_call(low, high, [(0, 1)], 0, (proj_in,), True)
        found = raw + lax.ppermute(raw, "mdl", swap)
        for k in range(low, high):
            back = [(z, (z - k) % experts) for z in range(experts)]
            codes.append(found[0] if k == 0 else lax.ppermute(found[k - low], "exp", back))

    made, total = [codes[0], raw[0]], None
    for j in range(count):
        last = j == count - 1
        turn, (x,) = ordered(turn, [mine[-1][j]], made, False) if j else (turn, [mine[-1][j]])
        args = [x, lax.ppermute(x, "mdl", swap), *weights]
        args += [] if total is None else [total]
        args += [proj_in] if last else []
        total = vmem_call(
            functools.partial(part_kernel, chunks[j], cuts, total is None, last),
            args,
            (rank, tokens.shape[0]) if last else (tokens.shape[0], 2 * gate.shape[1]),
            "part",
        )
    total = total + lax.ppermute(total, "mdl", swap)
    codes.append(lax.ppermute(total, "exp", ring))

    def grads(steps, more):
        vmem = pl.BlockSpec(memory_space=pltpu.VMEM)
        args = [grad_mine, grad_other, doc_ids, routes.T, *[codes[k] for k in steps], *more]
        return pl.pallas_call(
            functools.partial(grads_kernel, steps, experts),
            in_specs=[pl.BlockSpec(memory_space=pltpu.SMEM)] + [vmem] * len(args),
            out_specs=vmem,
            out_shape=jax.ShapeDtypeStruct((DOCS_DEV, experts, rank * rank), jnp.float32),
            scratch_shapes=[pltpu.VMEM((experts, rank, tokens.shape[0]), jnp.float32)],
            compiler_params=pltpu.CompilerParams(vmem_limit_bytes=4 * 2**20),
            cost_estimate=FREE,
            name="doc_grads",
        )(home.reshape(1), *args)

    first = grads(range(experts - 1), ())
    return grads(range(experts - 1, experts), (first,))


def solution(mesh):
    placed = (
        P(("grp", "exp", "dat"), "mdl"),
        P(("grp", "exp", "dat"), "mdl"),
        P(("grp", "exp", "dat"), None),
        P(("grp", "exp", "dat"), None),
        P("exp", "dat", "mdl"),
        P("exp", "dat", "mdl"),
        P(None, "mdl"),
        P(None, "mdl"),
    )
    return jax.shard_map(
        on_device,
        mesh=mesh,
        in_specs=placed,
        out_specs=P(("grp", "exp", "dat"), None, None),
        check_vma=False,
    )
```
